32 devices in a mesh: tm: 4 (over y, core), space: 8 (over z, x).
Axes of the slice: x: 2, y: 2, z: 4, core: 2. Of those that a mesh axis runs over, the one named last changes fastest.
Arguments:
- slab_states: float32 [4, 2, 64, 32, 512], P('tm', None, 'space'), may hold values from -6 to 6
- velocity: float32 [2, 3, 64, 32, 512], P(None, None, 'space'), may hold values from -0.9 to 0.9
- snap_of_step: int32 [4, 2], P('tm'), may hold values from 0 to 1
Outputs:
- slab_starts: float32 [4, 2, 64, 32, 512], P('tm', None, 'space')
- heater_grad: float32 [64, 32, 512], P('space', 'tm')
The draws below stay inside these ranges and needn't reach their ends.
All inputs are finite; a program needn't handle non-finite values.
Results may differ from the reference program's by a relative error of at most 0.00002.
Values sent between devices are 32-bit elements; how exact they have to be, the bound alone decides.
A program may use at most 64 MiB of HBM per device.

```python
import jax
import jax.numpy as jnp
from jax import lax

NY = 32
NZ = 512
STEPS = 2
SNAPS = 2
NX = 64
SLABS = 4


def place_ends(array, key, low, high):
    place = [jax.random.randint(jax.random.fold_in(key, axis), (), 0, length) for axis, length in enumerate(array.shape)]
    longest = array.shape.index(max(array.shape))
    next_to = place[:longest] + [(place[longest] + 1) % array.shape[longest]] + place[longest + 1:]
    return array.at[tuple(place)].set(low).at[tuple(next_to)].set(high)


def level_of(rng, shape, shards, smallest, top_value):
    loudness = 1.0
    for axis_at, shards_of in shards:
        draws = jax.random.uniform(jax.random.fold_in(jax.random.fold_in(rng, 6), axis_at), (shards_of,), jnp.float32, smallest / len(shards), top_value / len(shards))
        loudness = loudness * jnp.repeat(jnp.exp(draws), shape[axis_at] // shards_of).reshape((-1,) + (1,) * (len(shape) - 1 - axis_at))
    return loudness


def gaussian(key, extent, width, most, cuts=(), held_as=jnp.bfloat16):
    values = jax.random.normal(key, extent, jnp.float32) * width
    if len(cuts) > 0:
        values = level_of(key, extent, cuts, -0.22, 0.18) * values
    return jnp.clip(values, min=-most, max=most).astype(held_as)


def setup_inputs(seed: int = 0) -> dict:
    key_list = jax.random.split(jax.random.key(seed), 4)
    return {
        "slab_states": gaussian(key_list[0], (SLABS, 2, NX, NY, NZ), 1.0, 6.0, ((0, 4), (2, 8)), jnp.float32),
        "velocity": gaussian(key_list[1], (SNAPS, 3, NX, NY, NZ), 0.3, 0.9, ((2, 8),), jnp.float32),
        "snap_of_step": place_ends(jax.random.randint(key_list[2], (SLABS, STEPS), 0, SNAPS), jax.random.fold_in(key_list[2], 1), 0, SNAPS - 1).astype(jnp.int32),
    }


coupling = 0.3


def advance(widened, flow):
    centre = widened[:, 1:-1]
    east_side = widened[:, 2:]
    west_side = widened[:, :-2]
    north_side = jnp.pad(centre, ((0, 0), (0, 0), (0, 1), (0, 0)))[:, :, 1:]
    south_side = jnp.pad(centre, ((0, 0), (0, 0), (1, 0), (0, 0)))[:, :, :-1]
    upper_side = jnp.pad(centre, ((0, 0), (0, 0), (0, 0), (0, 1)))[:, :, :, 1:]
    lower_side = jnp.pad(centre, ((0, 0), (0, 0), (0, 0), (1, 0)))[:, :, :, :-1]
    laplace = east_side + west_side + north_side + south_side + upper_side + lower_side - 6.0 * centre
    transport = flow[0] * (east_side - west_side) + flow[1] * (north_side - south_side) + flow[2] * (upper_side - lower_side)
    temper = centre[0] + 0.14 * laplace[0] + 0.25 * transport[0] + coupling * centre[1]
    dopant = centre[1] + 0.06 * laplace[1] + 0.25 * transport[1]
    return jnp.stack([temper, dopant])


def sweep_slab(adjoint, flow_bank, snaps):
    total = jnp.zeros(adjoint.shape[1:], jnp.float32)
    for step_index in reversed(range(STEPS)):
        flow = lax.dynamic_index_in_dim(flow_bank, snaps[step_index], 0, keepdims=False)
        widened = jnp.pad(adjoint, ((0, 0), (1, 1), (0, 0), (0, 0)))
        adjoint = advance(widened, flow)
        total = total + adjoint[0]
    return adjoint, total


def reference(slab_states, velocity, snap_of_step):
    first = [sweep_slab(slab_states[slab_index], velocity, snap_of_step[slab_index])[0] for slab_index in range(SLABS)]
    carried = first[1:] + [slab_states[SLABS - 1]]
    starts = []
    grand = jnp.zeros(slab_states.shape[2:], jnp.float32)
    for slab_index in range(SLABS):
        result, total = sweep_slab(carried[slab_index], velocity, snap_of_step[slab_index])
        starts.append(result)
        grand = grand + total
    return jnp.stack(starts), grand / STEPS
```

```python
import functools

import jax
import jax.numpy as jnp
from jax import lax
from jax.experimental import pallas as pl
from jax.experimental.pallas import tpu as pltpu
from jax.sharding import PartitionSpec as P

coupling = 0.3
MESH = pl.DeviceIdType.MESH


def shifted(field):
    rows, lanes = field.shape
    row = lax.broadcasted_iota(jnp.int32, field.shape, 0)
    lane = lax.broadcasted_iota(jnp.int32, field.shape, 1)
    north = jnp.where(row == rows - 1, 0.0, pltpu.roll(field, rows - 1, 0))
    south = jnp.where(row == 0, 0.0, pltpu.roll(field, 1, 0))
    upper = jnp.where(lane == lanes - 1, 0.0, pltpu.roll(field, lanes - 1, 1))
    lower = jnp.where(lane == 0, 0.0, pltpu.roll(field, 1, 1))
    return north, south, upper, lower


def moved(west, centre, east, u, v, w, rate):
    north, south, upper, lower = shifted(centre)
    around = (east + west) + (north + south) + (upper + lower)
    transport = u * (east - west) + v * (north - south) + w * (upper - lower)
    return (1.0 - 6.0 * rate) * centre + rate * around + 0.25 * transport


def layer_step(src, flow, snap, layer):
    u, v, w = (flow[snap, c, layer] for c in range(3))
    a, b = src[0, layer + 1], src[1, layer + 1]
    temper = moved(src[0, layer], a, src[0, layer + 2], u, v, w, 0.14) + coupling * b
    dopant = moved(src[1, layer], b, src[1, layer + 2], u, v, w, 0.06)
    return temper, dopant


def kernel(
    slabs, blocks, state, velocity, snaps, out, grad,
    x0, x1, x2, y0, y1, y2, flow, total, from_mate, from_early, from_late,
    load_sem, halo_send, halo_recv, pass_send, pass_recv, grad_send, grad_recv, out_sem,
):
    t, s = lax.axis_index("tm"), lax.axis_index("space")
    depth = x2.shape[1]
    pairs = depth // 2
    steps = snaps.shape[1]
    has_up, has_down = s < blocks - 1, s > 0
    first_phase, second_phase = t > 0, t < slabs - 1

    load_state = pltpu.make_async_copy(state, x0.at[:, pl.ds(1, depth)], load_sem.at[0])
    load_flow = pltpu.make_async_copy(velocity, flow, load_sem.at[1])

    @pl.when(first_phase)
    def _():
        load_state.start()

    load_flow.start()

    barrier = pltpu.get_barrier_semaphore()

    def greet(target):
        pl.semaphore_signal(barrier, inc=1, device_id=target, device_id_type=MESH)

    for other in range(1, slabs):
        greet({"tm": lax.rem(t + other, slabs)})
    pl.when(has_up)(lambda: greet({"space": s + 1}))
    pl.when(has_down)(lambda: greet({"space": s - 1}))
    ends = jnp.where(has_up, 0, 1) + jnp.where(has_down, 0, 1)
    pl.semaphore_wait(barrier, slabs + 1 - ends)

    def halo(k, buf, source=None):
        low, high = (buf.at[:, 1], buf.at[:, depth]) if source is None else (source.at[:, 0], source.at[:, depth - 1])
        up = pltpu.make_async_remote_copy(
            high, buf.at[:, 0], halo_send.at[k, 0], halo_recv.at[k, 0], {"space": s + 1}, MESH)
        down = pltpu.make_async_remote_copy(
            low, buf.at[:, depth + 1], halo_send.at[k, 1], halo_recv.at[k, 1], {"space": s - 1}, MESH)
        return up, down

    def send_halo(pair):
        pl.when(has_up)(lambda: pair[0].start())
        pl.when(has_down)(lambda: pair[1].start())

    def recv_halo(pair):
        pl.when(has_down)(lambda: pair[0].wait_recv())
        pl.when(has_up)(lambda: pair[1].wait_recv())

    def sent_halo(pair):
        pl.when(has_up)(lambda: pair[0].wait_send())
        pl.when(has_down)(lambda: pair[1].wait_send())

    def clear_ends(*bufs):
        for buf in bufs:
            @pl.when(s == 0)
            def _(buf=buf):
                buf[:, 0] = jnp.zeros(buf.shape[:1] + buf.shape[2:], jnp.float32)

            @pl.when(s == blocks - 1)
            def _(buf=buf):
                buf[:, depth + 1] = jnp.zeros(buf.shape[:1] + buf.shape[2:], jnp.float32)

    halo0, halo1, halo2, halo3 = halo(0, x0, state), halo(1, x1), halo(2, y0), halo(3, y1)

    def passing(layer, target):
        return pltpu.make_async_remote_copy(
            x2.at[:, layer], y0.at[:, layer + 1], pass_send.at[layer], pass_recv.at[layer], {"tm": target}, MESH)

    def step_into(src, dst, offset, snap, p, summed=False):
        for layer in (p, depth - 1 - p):
            temper, dopant = layer_step(src, flow, snap, layer)
            dst[0, layer + offset] = temper
            dst[1, layer + offset] = dopant
            if summed:
                total[layer] = src[0, layer + 1] + temper

    @pl.when(first_phase)
    def _():
        send_halo(halo0)
        clear_ends(x0, x1)
        load_state.wait()

    load_flow.wait()

    @pl.when(first_phase)
    def _():
        @pl.loop(0, pairs)
        def _(i):
            p = pairs - 1 - i

            @pl.when(p == 0)
            def _():
                recv_halo(halo0)

            step_into(x0, x1, 1, snaps[0, steps - 1], p)

        send_halo(halo1)

        @pl.loop(0, pairs)
        def _(i):
            p = pairs - 1 - i

            @pl.when(p == 0)
            def _():
                recv_halo(halo1)

            step_into(x1, x2, 0, snaps[0, 0], p, summed=True)

            @pl.when(p == pairs - 1)
            def _():
                passing(p, t - 1).start()
                passing(depth - 1 - p, t - 1).start()

        @pl.loop(0, pairs - 1)
        def _(p):
            passing(p, t - 1).start()
            passing(depth - 1 - p, t - 1).start()

    @pl.when(second_phase)
    def _():
        clear_ends(y0, y1)

        def arrived(p):
            passing(p, t + 1).wait_recv()
            passing(depth - 1 - p, t + 1).wait_recv()

        arrived(0)
        send_halo(halo2)
        slow = t == 1

        @pl.when(jnp.logical_not(slow))
        def _():
            for p in range(1, pairs):
                arrived(p)

        @pl.loop(0, pairs)
        def _(i):
            p = lax.rem(i + jnp.where(slow, 0, 1), pairs)

            @pl.when(jnp.logical_and(slow, i < pairs - 1))
            def _():
                arrived(i + 1)

            @pl.when(p == 0)
            def _():
                recv_halo(halo2)

            step_into(y0, y1, 1, snaps[0, steps - 1], p)

            @pl.when(p == 0)
            def _():
                send_halo(halo3)

        @pl.loop(0, pairs)
        def _(i):
            p = pairs - 1 - i

            @pl.when(p == 0)
            def _():
                recv_halo(halo3)

            step_into(y1, y2, 0, snaps[0, 0], p, summed=True)

    store_mid = pltpu.make_async_copy(y2, out, out_sem)
    store_end = pltpu.make_async_copy(x2, out, out_sem)
    pl.when(second_phase)(lambda: store_mid.start())
    pl.when(t == slabs - 1)(lambda: store_end.start())

    rows = total.shape[1] // slabs

    def share(first, count, dst, slot, target):
        return pltpu.make_async_remote_copy(
            total.at[:, pl.ds(first * rows, count * rows)], dst, grad_send.at[target], grad_recv.at[slot],
            {"tm": target}, MESH)

    mate0 = share(1, 3, from_mate, 0, 1)
    mate3 = share(0, 3, from_mate, 0, 2)
    back1 = share(0, 1, from_late, 2, 0)
    back2 = share(3, 1, from_late, 2, 3)
    cross20 = share(0, 1, from_early, 1, 0)
    cross21 = share(1, 1, from_early, 1, 1)
    cross12 = share(2, 1, from_early, 1, 2)
    cross13 = share(3, 1, from_early, 1, 3)

    def mine(index):
        return total[:, index * rows:(index + 1) * rows]

    scale = 1.0 / steps

    @pl.when(t == 0)
    def _():
        mate0.start()
        cross20.wait_recv()
        back1.wait_recv()
        grad[...] = (mine(0) + from_late[...] + from_early[...]) * scale
        mate0.wait_send()

    @pl.when(t == 1)
    def _():
        mate0.wait_recv()
        total[:, rows:] += from_mate[...]
        cross12.start()
        cross13.start()
        back1.start()
        cross21.wait_recv()
        grad[...] = (mine(1) + from_early[...]) * scale
        cross12.wait_send()
        cross13.wait_send()
        back1.wait_send()

    @pl.when(t == 2)
    def _():
        mate3.wait_recv()
        total[:, :3 * rows] += from_mate[...]
        cross20.start()
        cross21.start()
        back2.start()
        cross12.wait_recv()
        grad[...] = (mine(2) + from_early[...]) * scale
        cross20.wait_send()
        cross21.wait_send()
        back2.wait_send()

    @pl.when(t == 3)
    def _():
        mate3.start()
        back2.wait_recv()
        cross13.wait_recv()
        grad[...] = (mine(3) + from_late[...] + from_early[...]) * scale
        mate3.wait_send()

    @pl.when(first_phase)
    def _():
        sent_halo(halo0)
        sent_halo(halo1)

        @pl.loop(0, depth)
        def _(layer):
            passing(layer, t - 1).wait_send()

    @pl.when(second_phase)
    def _():
        sent_halo(halo2)
        sent_halo(halo3)
        store_mid.wait()

    pl.when(t == slabs - 1)(lambda: store_end.wait())


def body(slabs, blocks, slab_states, velocity, snap_of_step):
    state = slab_states[0]
    fields, depth, ny, nz = state.shape
    rows = ny // slabs
    f32 = jnp.float32
    widened = pltpu.VMEM((fields, depth + 2, ny, nz), f32)
    plain = pltpu.VMEM((fields, depth, ny, nz), f32)
    dma = pltpu.SemaphoreType.DMA
    final, gradient = pl.pallas_call(
        functools.partial(kernel, slabs, blocks),
        out_shape=(
            jax.ShapeDtypeStruct(state.shape, f32),
            jax.ShapeDtypeStruct((depth, rows, nz), f32),
        ),
        in_specs=[
            pl.BlockSpec(memory_space=pl.ANY),
            pl.BlockSpec(memory_space=pl.ANY),
            pl.BlockSpec(memory_space=pltpu.SMEM),
        ],
        out_specs=(pl.BlockSpec(memory_space=pl.ANY), pl.BlockSpec(memory_space=pltpu.VMEM)),
        scratch_shapes=[
            widened, widened, plain, widened, widened, plain,
            pltpu.VMEM(velocity.shape, f32),
            pltpu.VMEM((depth, ny, nz), f32),
            pltpu.VMEM((depth, 3 * rows, nz), f32),
            pltpu.VMEM((depth, rows, nz), f32),
            pltpu.VMEM((depth, rows, nz), f32),
            dma((2,)), dma((4, 2)), dma((4, 2)), dma((depth,)), dma((depth,)), dma((slabs,)), dma((3,)), dma,
        ],
        compiler_params=pltpu.CompilerParams(
            collective_id=0, has_side_effects=True, vmem_limit_bytes=32 * 1024 * 1024),
        cost_estimate=pl.CostEstimate(flops=200 * state.size, bytes_accessed=28 * state.size, transcendentals=0),
    )(state, velocity, snap_of_step)
    return final[None], gradient


def solution(mesh):
    placed = (P("tm", None, "space", None, None), P(None, None, "space", None, None), P("tm", None))
    return jax.shard_map(
        functools.partial(body, mesh.shape["tm"], mesh.shape["space"]),
        mesh=mesh,
        in_specs=placed,
        out_specs=(P("tm", None, "space", None, None), P("space", "tm", None)),
        check_vma=False,
    )
```

```python
import functools

import jax
import jax.numpy as jnp
from jax import lax
from jax.experimental import pallas as pl
from jax.experimental.pallas import tpu as pltpu
from jax.sharding import PartitionSpec as P

coupling = 0.3
MESH = pl.DeviceIdType.MESH


def shifted(field):
    rows, lanes = field.shape
    row = lax.broadcasted_iota(jnp.int32, field.shape, 0)
    lane = lax.broadcasted_iota(jnp.int32, field.shape, 1)
    north = jnp.where(row == rows - 1, 0.0, pltpu.roll(field, rows - 1, 0))
    south = jnp.where(row == 0, 0.0, pltpu.roll(field, 1, 0))
    upper = jnp.where(lane == lanes - 1, 0.0, pltpu.roll(field, lanes - 1, 1))
    lower = jnp.where(lane == 0, 0.0, pltpu.roll(field, 1, 1))
    return north, south, upper, lower


def moved(west, centre, east, u, v, w, rate):
    north, south, upper, lower = shifted(centre)
    around = (east + west) + (north + south) + (upper + lower)
    transport = u * (east - west) + v * (north - south) + w * (upper - lower)
    return (1.0 - 6.0 * rate) * centre + rate * around + 0.25 * transport


def layer_step(src, flow, snap, layer):
    u, v, w = (flow[snap, c, layer] for c in range(3))
    a, b = src[0, layer + 1], src[1, layer + 1]
    temper = moved(src[0, layer], a, src[0, layer + 2], u, v, w, 0.14) + coupling * b
    dopant = moved(src[1, layer], b, src[1, layer + 2], u, v, w, 0.06)
    return temper, dopant


def kernel(
    slabs, blocks, state, velocity, snaps, out, grad,
    x0, x1, x2, y0, y1, y2, flow, total, from_mate, from_early, from_late,
    load_sem, halo_send, halo_recv, pass_send, pass_recv, grad_send, grad_recv, out_sem,
):
    t, s = lax.axis_index("tm"), lax.axis_index("space")
    depth = x2.shape[1]
    pairs = depth // 2
    steps = snaps.shape[1]
    has_up, has_down = s < blocks - 1, s > 0
    first_phase, second_phase = t > 0, t < slabs - 1

    load_state = pltpu.make_async_copy(state, x0.at[:, pl.ds(1, depth)], load_sem.at[0])
    load_flow = pltpu.make_async_copy(velocity, flow, load_sem.at[1])

    @pl.when(first_phase)
    def _():
        load_state.start()

    load_flow.start()

    barrier = pltpu.get_barrier_semaphore()

    def greet(target):
        pl.semaphore_signal(barrier, inc=1, device_id=target, device_id_type=MESH)

    for other in range(1, slabs):
        greet({"tm": lax.rem(t + other, slabs)})
    for by, there in ((1, has_up), (-1, has_down)):
        @pl.when(there)
        def _(by=by):
            greet({"space": s + by})
            pl.when(first_phase)(lambda: greet({"tm": t - 1, "space": s + by}))
            pl.when(second_phase)(lambda: greet({"tm": t + 1, "space": s + by}))

    sides = jnp.where(has_up, 1, 0) + jnp.where(has_down, 1, 0)
    rounds = 1 + jnp.where(first_phase, 1, 0) + jnp.where(second_phase, 1, 0)
    pl.semaphore_wait(barrier, slabs - 1 + sides * rounds)

    def halo(k, low, high, buf, to=0):
        def copy(source, layer, side, by):
            return pltpu.make_async_remote_copy(
                source, buf.at[:, layer], halo_send.at[k, side], halo_recv.at[k, side],
                {"tm": t + to, "space": s + by}, MESH)

        return copy(high, 0, 0, 1), copy(low, depth + 1, 1, -1)

    def send_halo(pair):
        pl.when(has_up)(lambda: pair[0].start())
        pl.when(has_down)(lambda: pair[1].start())

    def recv_halo(pair):
        pl.when(has_down)(lambda: pair[0].wait_recv())
        pl.when(has_up)(lambda: pair[1].wait_recv())

    def sent_halo(pair):
        pl.when(has_up)(lambda: pair[0].wait_send())
        pl.when(has_down)(lambda: pair[1].wait_send())

    def clear_ends(*bufs):
        for buf in bufs:
            @pl.when(s == 0)
            def _(buf=buf):
                buf[:, 0] = jnp.zeros(buf.shape[:1] + buf.shape[2:], jnp.float32)

            @pl.when(s == blocks - 1)
            def _(buf=buf):
                buf[:, depth + 1] = jnp.zeros(buf.shape[:1] + buf.shape[2:], jnp.float32)

    halo0 = halo(0, state.at[:, 0], state.at[:, depth - 1], x0)
    halo1 = halo(1, x1.at[:, 1], x1.at[:, depth], x1)
    halo2 = halo(2, x2.at[:, 0], x2.at[:, depth - 1], y0, -1)
    halo3 = halo(3, y1.at[:, 1], y1.at[:, depth], y1)

    def passing(layer, target):
        return pltpu.make_async_remote_copy(
            x2.at[:, layer], y0.at[:, layer + 1], pass_send.at[layer], pass_recv.at[layer], {"tm": target}, MESH)

    def step_into(src, dst, offset, snap, p, summed=False):
        for layer in (p, depth - 1 - p):
            temper, dopant = layer_step(src, flow, snap, layer)
            dst[0, layer + offset] = temper
            dst[1, layer + offset] = dopant
            if summed:
                total[layer] = src[0, layer + 1] + temper

    @pl.when(first_phase)
    def _():
        send_halo(halo0)
        clear_ends(x0, x1)
        load_state.wait()

    load_flow.wait()

    @pl.when(first_phase)
    def _():
        @pl.loop(0, pairs)
        def _(i):
            p = pairs - 1 - i

            @pl.when(p == 0)
            def _():
                recv_halo(halo0)

            step_into(x0, x1, 1, snaps[0, steps - 1], p)

        send_halo(halo1)

        @pl.loop(0, pairs)
        def _(i):
            p = pairs - 1 - i

            @pl.when(p == 0)
            def _():
                recv_halo(halo1)

            step_into(x1, x2, 0, snaps[0, 0], p, summed=True)

            @pl.when(p == pairs - 1)
            def _():
                passing(p, t - 1).start()
                passing(depth - 1 - p, t - 1).start()

        send_halo(halo2)

        @pl.loop(0, pairs - 1)
        def _(p):
            passing(p, t - 1).start()
            passing(depth - 1 - p, t - 1).start()

    rows = total.shape[1] // slabs
    parts = ((1, depth - 2), (0, 1), (depth - 1, 1))
    inner, outer = (0,), (1, 2)

    class Share:
        def __init__(self, first, count, dst, slot, target):
            self.copies = [
                pltpu.make_async_remote_copy(
                    total.at[pl.ds(layer, layers), pl.ds(first * rows, count * rows)],
                    dst.at[pl.ds(layer, layers)], grad_send.at[target, part], grad_recv.at[slot, part],
                    {"tm": target}, MESH)
                for part, (layer, layers) in enumerate(parts)
            ]

        def start(self, which=inner + outer):
            for part in which:
                self.copies[part].start()

        def wait_recv(self):
            for copy in self.copies:
                copy.wait_recv()

        def wait_send(self):
            for copy in self.copies:
                copy.wait_send()

    mate0 = Share(1, 3, from_mate, 0, 1)
    mate3 = Share(0, 3, from_mate, 0, 2)
    back1 = Share(0, 1, from_late, 2, 0)
    back2 = Share(3, 1, from_late, 2, 3)
    cross20 = Share(0, 1, from_early, 1, 0)
    cross21 = Share(1, 1, from_early, 1, 1)
    cross12 = Share(2, 1, from_early, 1, 2)
    cross13 = Share(3, 1, from_early, 1, 3)

    def give(which):
        @pl.when(t == 0)
        def _():
            mate0.start(which)

        @pl.when(t == 1)
        def _():
            if which == inner:
                mate0.wait_recv()
            for layer, layers in (parts[part] for part in which):
                total[layer:layer + layers, rows:] += from_mate[layer:layer + layers]
            for each in (cross12, cross13, back1):
                each.start(which)

        @pl.when(t == 2)
        def _():
            if which == inner:
                mate3.wait_recv()
            for layer, layers in (parts[part] for part in which):
                total[layer:layer + layers, :3 * rows] += from_mate[layer:layer + layers]
            for each in (cross20, cross21, back2):
                each.start(which)

    pl.when(t == slabs - 1)(lambda: mate3.start())

    @pl.when(second_phase)
    def _():
        clear_ends(y0, y1)

        def arrived(p):
            passing(p, t + 1).wait_recv()
            passing(depth - 1 - p, t + 1).wait_recv()

        arrived(0)
        slow = t == 1

        @pl.when(jnp.logical_not(slow))
        def _():
            for p in range(1, pairs):
                arrived(p)

        @pl.loop(0, pairs)
        def _(i):
            p = lax.rem(i + jnp.where(slow, 0, 1), pairs)

            @pl.when(jnp.logical_and(slow, i < pairs - 1))
            def _():
                arrived(i + 1)

            @pl.when(p == 0)
            def _():
                recv_halo(halo2)

            step_into(y0, y1, 1, snaps[0, steps - 1], p)

            @pl.when(p == 0)
            def _():
                send_halo(halo3)

        @pl.loop(0, pairs)
        def _(i):
            p = pairs - 1 - i

            @pl.when(p == 0)
            def _():
                give(inner)
                recv_halo(halo3)

            step_into(y1, y2, 0, snaps[0, 0], p, summed=True)

        give(outer)

    store_mid = pltpu.make_async_copy(y2, out, out_sem)
    store_end = pltpu.make_async_copy(x2, out, out_sem)
    pl.when(second_phase)(lambda: store_mid.start())
    pl.when(t == slabs - 1)(lambda: store_end.start())

    def mine(index):
        return total[:, index * rows:(index + 1) * rows]

    scale = 1.0 / steps

    @pl.when(t == 0)
    def _():
        cross20.wait_recv()
        back1.wait_recv()
        grad[...] = (mine(0) + from_late[...] + from_early[...]) * scale
        mate0.wait_send()

    @pl.when(t == 1)
    def _():
        cross21.wait_recv()
        grad[...] = (mine(1) + from_early[...]) * scale
        cross12.wait_send()
        cross13.wait_send()
        back1.wait_send()

    @pl.when(t == 2)
    def _():
        cross12.wait_recv()
        grad[...] = (mine(2) + from_early[...]) * scale
        cross20.wait_send()
        cross21.wait_send()
        back2.wait_send()

    @pl.when(t == 3)
    def _():
        back2.wait_recv()
        cross13.wait_recv()
        grad[...] = (mine(3) + from_late[...] + from_early[...]) * scale
        mate3.wait_send()

    @pl.when(first_phase)
    def _():
        sent_halo(halo0)
        sent_halo(halo1)
        sent_halo(halo2)

        @pl.loop(0, depth)
        def _(layer):
            passing(layer, t - 1).wait_send()

    @pl.when(second_phase)
    def _():
        sent_halo(halo3)
        store_mid.wait()

    pl.when(t == slabs - 1)(lambda: store_end.wait())


def body(slabs, blocks, slab_states, velocity, snap_of_step):
    state = slab_states[0]
    fields, depth, ny, nz = state.shape
    rows = ny // slabs
    f32 = jnp.float32
    widened = pltpu.VMEM((fields, depth + 2, ny, nz), f32)
    plain = pltpu.VMEM((fields, depth, ny, nz), f32)
    dma = pltpu.SemaphoreType.DMA
    final, gradient = pl.pallas_call(
        functools.partial(kernel, slabs, blocks),
        out_shape=(
            jax.ShapeDtypeStruct(state.shape, f32),
            jax.ShapeDtypeStruct((depth, rows, nz), f32),
        ),
        in_specs=[
            pl.BlockSpec(memory_space=pl.ANY),
            pl.BlockSpec(memory_space=pl.ANY),
            pl.BlockSpec(memory_space=pltpu.SMEM),
        ],
        out_specs=(pl.BlockSpec(memory_space=pl.ANY), pl.BlockSpec(memory_space=pltpu.VMEM)),
        scratch_shapes=[
            widened, widened, plain, widened, widened, plain,
            pltpu.VMEM(velocity.shape, f32),
            pltpu.VMEM((depth, ny, nz), f32),
            pltpu.VMEM((depth, 3 * rows, nz), f32),
            pltpu.VMEM((depth, rows, nz), f32),
            pltpu.VMEM((depth, rows, nz), f32),
            dma((2,)), dma((4, 2)), dma((4, 2)), dma((depth,)), dma((depth,)), dma((slabs, 3)), dma((3, 3)), dma,
        ],
        compiler_params=pltpu.CompilerParams(
            collective_id=0, has_side_effects=True, vmem_limit_bytes=60 * 1024 * 1024),
        cost_estimate=pl.CostEstimate(flops=200 * state.size, bytes_accessed=28 * state.size, transcendentals=0),
    )(state, velocity, snap_of_step)
    return final[None], gradient


def solution(mesh):
    placed = (P("tm", None, "space", None, None), P(None, None, "space", None, None), P("tm", None))
    return jax.shard_map(
        functools.partial(body, mesh.shape["tm"], mesh.shape["space"]),
        mesh=mesh,
        in_specs=placed,
        out_specs=(P("tm", None, "space", None, None), P("space", "tm", None)),
        check_vma=False,
    )
```

```python
import functools

import jax
import jax.numpy as jnp
from jax import lax
from jax.experimental import pallas as pl
from jax.experimental.pallas import tpu as pltpu
from jax.sharding import PartitionSpec as P

coupling = 0.3
MESH = pl.DeviceIdType.MESH


def shifted(field):
    rows, lanes = field.shape
    row = lax.broadcasted_iota(jnp.int32, field.shape, 0)
    lane = lax.broadcasted_iota(jnp.int32, field.shape, 1)
    north = jnp.where(row == rows - 1, 0.0, pltpu.roll(field, rows - 1, 0))
    south = jnp.where(row == 0, 0.0, pltpu.roll(field, 1, 0))
    upper = jnp.where(lane == lanes - 1, 0.0, pltpu.roll(field, lanes - 1, 1))
    lower = jnp.where(lane == 0, 0.0, pltpu.roll(field, 1, 1))
    return north, south, upper, lower


def moved(west, centre, east, u, v, w, rate):
    north, south, upper, lower = shifted(centre)
    around = (east + west) + (north + south) + (upper + lower)
    transport = u * (east - west) + v * (north - south) + w * (upper - lower)
    return (1.0 - 6.0 * rate) * centre + rate * around + 0.25 * transport


def flow_at(flow, snap, layer):
    return tuple(flow[snap, c, layer] for c in range(3))


def flow_picked(flow, pick, layer):
    rows, lanes = flow.shape[3:]
    pick = jnp.concatenate([pick] * (lanes // pick.shape[1]), axis=1)
    pick = jnp.concatenate([pick] * (rows // pick.shape[0]), axis=0)
    return tuple(jnp.where(pick > 0.5, flow[1, c, layer], flow[0, c, layer]) for c in range(3))


def temper_step(src, flows, layer):
    a, b = src[0, layer + 1], src[1, layer + 1]
    return moved(src[0, layer], a, src[0, layer + 2], *flows, 0.14) + coupling * b


def dopant_step(src, flows, layer):
    return moved(src[1, layer], src[1, layer + 1], src[1, layer + 2], *flows, 0.06)


def kernel(
    slabs, blocks, state, velocity, snaps_in, out, grad,
    x0, x1, x2, y0, y1, y2, flow, total, from_mate, from_early, from_late, snaps, pick_out, pick,
    load_sem, halo_send, halo_recv, pass_send, pass_recv, raw_send, raw_recv, grad_send, grad_recv, out_sem,
):
    t, s = lax.axis_index("tm"), lax.axis_index("space")
    depth = x2.shape[1]
    pairs = depth // 2
    steps = snaps.shape[1]
    has_up, has_down = s < blocks - 1, s > 0
    first_phase, second_phase = t > 0, t < slabs - 1
    mate = t + 1 - 2 * lax.rem(t, 2)
    source = slabs // 2

    load_state = pltpu.make_async_copy(state, x0.at[:, pl.ds(1, depth)], load_sem.at[0])
    load_flow = pltpu.make_async_copy(velocity, flow, load_sem.at[1])
    load_snaps = pltpu.make_async_copy(snaps_in, snaps, load_sem.at[2])

    load_snaps.start()

    @pl.when(first_phase)
    def _():
        load_state.start()

    load_flow.start()

    barrier = pltpu.get_barrier_semaphore()

    def greet(target):
        pl.semaphore_signal(barrier, inc=1, device_id=target, device_id_type=MESH)

    for other in range(1, slabs):
        greet({"tm": lax.rem(t + other, slabs)})
    for by, there in ((1, has_up), (-1, has_down)):
        @pl.when(there)
        def _(by=by):
            greet({"space": s + by})
            pl.when(first_phase)(lambda: greet({"tm": t - 1, "space": s + by}))
            pl.when(second_phase)(lambda: greet({"tm": t + 1, "space": s + by}))

    sides = jnp.where(has_up, 1, 0) + jnp.where(has_down, 1, 0)
    rounds = 1 + jnp.where(first_phase, 1, 0) + jnp.where(second_phase, 1, 0)
    pl.semaphore_wait(barrier, slabs - 1 + sides * rounds)

    def halo(k, field, low, high, buf, tm=t):
        def copy(source, layer, side, by):
            return pltpu.make_async_remote_copy(
                source, buf.at[field, layer], halo_send.at[k, field, side], halo_recv.at[k, field, side],
                {"tm": tm, "space": s + by}, MESH)

        return copy(high, 0, 0, 1), copy(low, depth + 1, 1, -1)

    def send_halo(pair):
        pl.when(has_up)(lambda: pair[0].start())
        pl.when(has_down)(lambda: pair[1].start())

    def recv_halo(pair):
        pl.when(has_down)(lambda: pair[0].wait_recv())
        pl.when(has_up)(lambda: pair[1].wait_recv())

    def sent_halo(pair):
        pl.when(has_up)(lambda: pair[0].wait_send())
        pl.when(has_down)(lambda: pair[1].wait_send())

    def clear_ends(*bufs):
        for buf in bufs:
            @pl.when(s == 0)
            def _(buf=buf):
                buf[:, 0] = jnp.zeros(buf.shape[:1] + buf.shape[2:], jnp.float32)

            @pl.when(s == blocks - 1)
            def _(buf=buf):
                buf[:, depth + 1] = jnp.zeros(buf.shape[:1] + buf.shape[2:], jnp.float32)

    A, B = 0, 1
    halo0 = [halo(0, f, state.at[f, 0], state.at[f, depth - 1], x0) for f in (A, B)]
    relay0 = halo(0, B, x0.at[B, 1], x0.at[B, depth], x0)
    halo1 = [halo(1, f, x1.at[f, 1], x1.at[f, depth], x1) for f in (A, B)]
    halo2 = [halo(2, f, x2.at[f, 0], x2.at[f, depth - 1], y0, (t - 1, mate)[f]) for f in (A, B)]
    halo3 = [halo(3, f, y1.at[f, 1], y1.at[f, depth], y1) for f in (A, B)]

    def passing(field, layer, target):
        return pltpu.make_async_remote_copy(
            x2.at[field, layer], y0.at[field, layer + 1], pass_send.at[field, layer], pass_recv.at[field, layer],
            {"tm": target}, MESH)

    def pass_pair(field, p, target):
        passing(field, p, target).start()
        passing(field, depth - 1 - p, target).start()

    def arrived(field, p, origin):
        passing(field, p, origin).wait_recv()
        passing(field, depth - 1 - p, origin).wait_recv()

    def raw(part, layer, layers):
        return pltpu.make_async_remote_copy(
            state.at[B, pl.ds(layer, layers)], x0.at[B, pl.ds(layer + 1, layers)],
            raw_send.at[part], raw_recv.at[part], {"tm": 0}, MESH)

    raws = [raw(0, 0, 1), raw(1, depth - 1, 1), raw(2, 1, depth - 2)]
    send_pick = pltpu.make_async_remote_copy(pick_out, pick, raw_send.at[3], raw_recv.at[3], {"tm": 0}, MESH)

    def step_into(src, dst, offset, snap, p, summed=False):
        for layer in (p, depth - 1 - p):
            flows = flow_at(flow, snap, layer)
            temper = temper_step(src, flows, layer)
            dst[A, layer + offset] = temper
            dst[B, layer + offset] = dopant_step(src, flows, layer)
            if summed:
                total[layer] = src[A, layer + 1] + temper

    @pl.when(first_phase)
    def _():
        send_halo(halo0[A])
        send_halo(halo0[B])

    load_snaps.wait()

    @pl.when(t == source)
    def _():
        for i in range(steps):
            pick_out[i] = jnp.full(pick_out.shape[1:], snaps[0, i].astype(jnp.float32))
        send_pick.start()
        for each in raws:
            each.start()

    clear_ends(x0, x1)
    pl.when(first_phase)(lambda: load_state.wait())
    load_flow.wait()

    @pl.when(t == 0)
    def _():
        raws[0].wait_recv()
        raws[1].wait_recv()
        send_halo(relay0)
        send_pick.wait_recv()
        raws[2].wait_recv()

        @pl.loop(0, pairs)
        def _(i):
            p = pairs - 1 - i

            @pl.when(p == 0)
            def _():
                recv_halo(relay0)

            for layer in (p, depth - 1 - p):
                x1[B, layer + 1] = dopant_step(x0, flow_picked(flow, pick[steps - 1], layer), layer)

        send_halo(halo1[B])

        @pl.loop(0, pairs)
        def _(i):
            p = pairs - 1 - i

            @pl.when(p == 0)
            def _():
                recv_halo(halo1[B])

            for layer in (p, depth - 1 - p):
                x2[B, layer] = dopant_step(x1, flow_picked(flow, pick[0], layer), layer)

        send_halo(halo2[B])
        for p in range(pairs):
            pass_pair(B, p, mate)

    @pl.when(first_phase)
    def _():
        @pl.loop(0, pairs)
        def _(i):
            p = pairs - 1 - i

            @pl.when(p == 0)
            def _():
                recv_halo(halo0[A])
                recv_halo(halo0[B])

            step_into(x0, x1, 1, snaps[0, steps - 1], p)

        send_halo(halo1[A])
        pl.when(t != source)(lambda: send_halo(halo1[B]))

        @pl.loop(0, pairs)
        def _(i):
            p = pairs - 1 - i

            @pl.when(p == 0)
            def _():
                recv_halo(halo1[A])
                pl.when(t != source)(lambda: recv_halo(halo1[B]))

            for layer in (p, depth - 1 - p):
                flows = flow_at(flow, snaps[0, 0], layer)
                temper = temper_step(x1, flows, layer)
                x2[A, layer] = temper
                total[layer] = x1[A, layer + 1] + temper

            @pl.when(t != source)
            def _():
                for layer in (p, depth - 1 - p):
                    x2[B, layer] = dopant_step(x1, flow_at(flow, snaps[0, 0], layer), layer)

            @pl.when(p == pairs - 1)
            def _():
                pass_pair(A, p, t - 1)

        send_halo(halo2[A])
        pl.when(t != source)(lambda: send_halo(halo2[B]))

        @pl.loop(0, pairs - 1)
        def _(p):
            pass_pair(A, p, t - 1)

        @pl.when(t != source)
        def _():
            @pl.loop(0, pairs)
            def _(p):
                pass_pair(B, p, mate)

    rows = total.shape[1] // slabs
    parts = ((1, depth - 2), (0, 1), (depth - 1, 1))
    inner, outer = (0,), (1, 2)

    class Share:
        def __init__(self, first, count, dst, slot, target):
            self.copies = [
                pltpu.make_async_remote_copy(
                    total.at[pl.ds(layer, layers), pl.ds(first * rows, count * rows)],
                    dst.at[pl.ds(layer, layers)], grad_send.at[target, part], grad_recv.at[slot, part],
                    {"tm": target}, MESH)
                for part, (layer, layers) in enumerate(parts)
            ]

        def start(self, which=inner + outer):
            for part in which:
                self.copies[part].start()

        def wait_recv(self):
            for copy in self.copies:
                copy.wait_recv()

        def wait_send(self):
            for copy in self.copies:
                copy.wait_send()

    mate0 = Share(1, 3, from_mate, 0, 1)
    mate3 = Share(0, 3, from_mate, 0, 2)
    back1 = Share(0, 1, from_late, 2, 0)
    back2 = Share(3, 1, from_late, 2, 3)
    cross20 = Share(0, 1, from_early, 1, 0)
    cross21 = Share(1, 1, from_early, 1, 1)
    cross12 = Share(2, 1, from_early, 1, 2)
    cross13 = Share(3, 1, from_early, 1, 3)

    def give(which):
        @pl.when(t == 0)
        def _():
            mate0.start(which)

        @pl.when(t == 1)
        def _():
            if which == inner:
                mate0.wait_recv()
            for layer, layers in (parts[part] for part in which):
                total[layer:layer + layers, rows:] += from_mate[layer:layer + layers]
            for each in (cross12, cross13, back1):
                each.start(which)

        @pl.when(t == 2)
        def _():
            if which == inner:
                mate3.wait_recv()
            for layer, layers in (parts[part] for part in which):
                total[layer:layer + layers, :3 * rows] += from_mate[layer:layer + layers]
            for each in (cross20, cross21, back2):
                each.start(which)

    pl.when(t == slabs - 1)(lambda: mate3.start())

    @pl.when(second_phase)
    def _():
        clear_ends(y0, y1)

        slow = t == source - 1

        for p in range(pairs):
            arrived(B, p, mate)

        arrived(A, 0, t + 1)

        @pl.when(jnp.logical_not(slow))
        def _():
            for p in range(1, pairs):
                arrived(A, p, t + 1)

        @pl.loop(0, pairs)
        def _(i):
            p = lax.rem(i + jnp.where(slow, 0, 1), pairs)

            @pl.when(jnp.logical_and(slow, i < pairs - 1))
            def _():
                arrived(A, i + 1, t + 1)

            @pl.when(p == 0)
            def _():
                recv_halo(halo2[A])
                recv_halo(halo2[B])

            step_into(y0, y1, 1, snaps[0, steps - 1], p)

            @pl.when(p == 0)
            def _():
                send_halo(halo3[A])
                send_halo(halo3[B])

        @pl.loop(0, pairs)
        def _(i):
            p = pairs - 1 - i

            @pl.when(p == 0)
            def _():
                give(inner)
                recv_halo(halo3[A])
                recv_halo(halo3[B])

            step_into(y1, y2, 0, snaps[0, 0], p, summed=True)

        give(outer)

    store_mid = pltpu.make_async_copy(y2, out, out_sem)
    store_end = pltpu.make_async_copy(x2, out, out_sem)
    pl.when(second_phase)(lambda: store_mid.start())
    pl.when(t == slabs - 1)(lambda: store_end.start())

    def mine(index):
        return total[:, index * rows:(index + 1) * rows]

    scale = 1.0 / steps

    @pl.when(t == 0)
    def _():
        cross20.wait_recv()
        back1.wait_recv()
        grad[...] = (mine(0) + from_late[...] + from_early[...]) * scale
        mate0.wait_send()

    @pl.when(t == 1)
    def _():
        cross21.wait_recv()
        grad[...] = (mine(1) + from_early[...]) * scale
        cross12.wait_send()
        cross13.wait_send()
        back1.wait_send()

    @pl.when(t == 2)
    def _():
        cross12.wait_recv()
        grad[...] = (mine(2) + from_early[...]) * scale
        cross20.wait_send()
        cross21.wait_send()
        back2.wait_send()

    @pl.when(t == 3)
    def _():
        back2.wait_recv()
        cross13.wait_recv()
        grad[...] = (mine(3) + from_late[...] + from_early[...]) * scale
        mate3.wait_send()

    @pl.when(t == 0)
    def _():
        sent_halo(relay0)

    @pl.when(t == source)
    def _():
        send_pick.wait_send()
        for each in raws:
            each.wait_send()

    @pl.when(first_phase)
    def _():
        for each in (halo0[A], halo0[B], halo1[A], halo2[A]):
            sent_halo(each)

        @pl.loop(0, depth)
        def _(layer):
            passing(A, layer, t - 1).wait_send()

    @pl.when(t != source)
    def _():
        sent_halo(halo1[B])
        sent_halo(halo2[B])

        @pl.loop(0, depth)
        def _(layer):
            passing(B, layer, mate).wait_send()

    @pl.when(second_phase)
    def _():
        sent_halo(halo3[A])
        sent_halo(halo3[B])
        store_mid.wait()

    pl.when(t == slabs - 1)(lambda: store_end.wait())


def body(slabs, blocks, slab_states, velocity, snap_of_step):
    state = slab_states[0]
    fields, depth, ny, nz = state.shape
    rows = ny // slabs
    f32 = jnp.float32
    widened = pltpu.VMEM((fields, depth + 2, ny, nz), f32)
    plain = pltpu.VMEM((fields, depth, ny, nz), f32)
    dma = pltpu.SemaphoreType.DMA
    final, gradient = pl.pallas_call(
        functools.partial(kernel, slabs, blocks),
        out_shape=(
            jax.ShapeDtypeStruct(state.shape, f32),
            jax.ShapeDtypeStruct((depth, rows, nz), f32),
        ),
        in_specs=[
            pl.BlockSpec(memory_space=pltpu.HBM),
            pl.BlockSpec(memory_space=pltpu.HBM),
            pl.BlockSpec(memory_space=pltpu.HBM),
        ],
        out_specs=(pl.BlockSpec(memory_space=pl.ANY), pl.BlockSpec(memory_space=pltpu.VMEM)),
        scratch_shapes=[
            widened, widened, plain, widened, widened, plain,
            pltpu.VMEM(velocity.shape, f32),
            pltpu.VMEM((depth, ny, nz), f32),
            pltpu.VMEM((depth, 3 * rows, nz), f32),
            pltpu.VMEM((depth, rows, nz), f32),
            pltpu.VMEM((depth, rows, nz), f32),
            pltpu.SMEM(snap_of_step.shape, jnp.int32),
            pltpu.VMEM((snap_of_step.shape[1], 8, 128), f32),
            pltpu.VMEM((snap_of_step.shape[1], 8, 128), f32),
            dma((3,)), dma((4, 2, 2)), dma((4, 2, 2)), dma((fields, depth)), dma((fields, depth)), dma((4,)), dma((4,)),
            dma((slabs, 3)), dma((3, 3)), dma,
        ],
        compiler_params=pltpu.CompilerParams(
            collective_id=0, has_side_effects=True, vmem_limit_bytes=32 * 1024 * 1024),
        cost_estimate=pl.CostEstimate(flops=200 * state.size, bytes_accessed=28 * state.size, transcendentals=0),
    )(state, velocity, snap_of_step)
    return final[None], gradient


def solution(mesh):
    placed = (P("tm", None, "space", None, None), P(None, None, "space", None, None), P("tm", None))
    return jax.shard_map(
        functools.partial(body, mesh.shape["tm"], mesh.shape["space"]),
        mesh=mesh,
        in_specs=placed,
        out_specs=(P("tm", None, "space", None, None), P("space", "tm", None)),
        check_vma=False,
    )
```

```python
import functools

import jax
import jax.numpy as jnp
from jax import lax
from jax.experimental import pallas as pl
from jax.experimental.pallas import tpu as pltpu
from jax.sharding import PartitionSpec as P

coupling = 0.3
MESH = pl.DeviceIdType.MESH


def shifted(field):
    rows, lanes = field.shape
    row = lax.broadcasted_iota(jnp.int32, field.shape, 0)
    lane = lax.broadcasted_iota(jnp.int32, field.shape, 1)
    north = jnp.where(row == rows - 1, 0.0, pltpu.roll(field, rows - 1, 0))
    south = jnp.where(row == 0, 0.0, pltpu.roll(field, 1, 0))
    upper = jnp.where(lane == lanes - 1, 0.0, pltpu.roll(field, lanes - 1, 1))
    lower = jnp.where(lane == 0, 0.0, pltpu.roll(field, 1, 1))
    return north, south, upper, lower


def moved(west, centre, east, u, v, w, rate):
    north, south, upper, lower = shifted(centre)
    around = (east + west) + (north + south) + (upper + lower)
    transport = u * (east - west) + v * (north - south) + w * (upper - lower)
    return (1.0 - 6.0 * rate) * centre + rate * around + 0.25 * transport


def flow_at(flow, snap, layer):
    return tuple(flow[snap, c, layer] for c in range(3))


def flow_picked(flow, pick, layer):
    rows, lanes = flow.shape[3:]
    pick = jnp.concatenate([pick] * (lanes // pick.shape[1]), axis=1)
    pick = jnp.concatenate([pick] * (rows // pick.shape[0]), axis=0)
    return tuple(jnp.where(pick > 0.5, flow[1, c, layer], flow[0, c, layer]) for c in range(3))


def temper_step(src, flows, layer):
    a, b = src[0, layer + 1], src[1, layer + 1]
    return moved(src[0, layer], a, src[0, layer + 2], *flows, 0.14) + coupling * b


def dopant_step(src, flows, layer):
    return moved(src[1, layer], src[1, layer + 1], src[1, layer + 2], *flows, 0.06)


def kernel(
    slabs, blocks, state, velocity, snaps_in, out, grad,
    x0, x1, x2, y0, y1, y2, flow, total, from_mate, from_early, from_late, snaps, pick_out, pick,
    load_sem, halo_send, halo_recv, pass_send, pass_recv, raw_send, raw_recv, grad_send, grad_recv, out_sem,
):
    t, s = lax.axis_index("tm"), lax.axis_index("space")
    depth = x2.shape[1]
    pairs = depth // 2
    steps = snaps.shape[1]
    has_up, has_down = s < blocks - 1, s > 0
    first_phase, second_phase = t > 0, t < slabs - 1
    mate = t + 1 - 2 * lax.rem(t, 2)
    source = slabs // 2

    load_state = pltpu.make_async_copy(state, x0.at[:, pl.ds(1, depth)], load_sem.at[0])
    load_flow = pltpu.make_async_copy(velocity, flow, load_sem.at[1])
    load_snaps = pltpu.make_async_copy(snaps_in, snaps, load_sem.at[2])

    load_snaps.start()

    @pl.when(first_phase)
    def _():
        load_state.start()

    load_flow.start()

    barrier = pltpu.get_barrier_semaphore()

    def greet(target):
        pl.semaphore_signal(barrier, inc=1, device_id=target, device_id_type=MESH)

    for other in range(1, slabs):
        greet({"tm": lax.rem(t + other, slabs)})
    for by, there in ((1, has_up), (-1, has_down)):
        @pl.when(there)
        def _(by=by):
            greet({"space": s + by})
            pl.when(first_phase)(lambda: greet({"tm": t - 1, "space": s + by}))
            pl.when(second_phase)(lambda: greet({"tm": t + 1, "space": s + by}))

    sides = jnp.where(has_up, 1, 0) + jnp.where(has_down, 1, 0)
    rounds = 1 + jnp.where(first_phase, 1, 0) + jnp.where(second_phase, 1, 0)
    pl.semaphore_wait(barrier, slabs - 1 + sides * rounds)

    def halo(k, field, low, high, buf, tm=t):
        def copy(source, layer, side, by):
            return pltpu.make_async_remote_copy(
                source, buf.at[field, layer], halo_send.at[k, field, side], halo_recv.at[k, field, side],
                {"tm": tm, "space": s + by}, MESH)

        return copy(high, 0, 0, 1), copy(low, depth + 1, 1, -1)

    def send_halo(pair):
        pl.when(has_up)(lambda: pair[0].start())
        pl.when(has_down)(lambda: pair[1].start())

    def recv_halo(pair):
        pl.when(has_down)(lambda: pair[0].wait_recv())
        pl.when(has_up)(lambda: pair[1].wait_recv())

    def sent_halo(pair):
        pl.when(has_up)(lambda: pair[0].wait_send())
        pl.when(has_down)(lambda: pair[1].wait_send())

    def clear_ends(*bufs):
        for buf in bufs:
            @pl.when(s == 0)
            def _(buf=buf):
                buf[:, 0] = jnp.zeros(buf.shape[:1] + buf.shape[2:], jnp.float32)

            @pl.when(s == blocks - 1)
            def _(buf=buf):
                buf[:, depth + 1] = jnp.zeros(buf.shape[:1] + buf.shape[2:], jnp.float32)

    A, B = 0, 1
    halo0 = [halo(0, f, state.at[f, 0], state.at[f, depth - 1], x0) for f in (A, B)]
    relay0 = halo(0, B, x0.at[B, 1], x0.at[B, depth], x0)
    halo1 = [halo(1, f, x1.at[f, 1], x1.at[f, depth], x1) for f in (A, B)]
    halo2 = [halo(2, f, x2.at[f, 0], x2.at[f, depth - 1], y0, (t - 1, mate)[f]) for f in (A, B)]
    halo3 = [halo(3, f, y1.at[f, 1], y1.at[f, depth], y1) for f in (A, B)]

    def passing(field, layer, target):
        return pltpu.make_async_remote_copy(
            x2.at[field, layer], y0.at[field, layer + 1], pass_send.at[field, layer], pass_recv.at[field, layer],
            {"tm": target}, MESH)

    def pass_pair(field, p, target):
        passing(field, p, target).start()
        passing(field, depth - 1 - p, target).start()

    def arrived(field, p, origin):
        passing(field, p, origin).wait_recv()
        passing(field, depth - 1 - p, origin).wait_recv()

    def raw(part, layer, layers):
        return pltpu.make_async_remote_copy(
            state.at[B, pl.ds(layer, layers)], x0.at[B, pl.ds(layer + 1, layers)],
            raw_send.at[part], raw_recv.at[part], {"tm": 0}, MESH)

    raws = [raw(0, 0, 1), raw(1, depth - 1, 1), raw(2, 1, depth - 2)]
    send_pick = pltpu.make_async_remote_copy(pick_out, pick, raw_send.at[3], raw_recv.at[3], {"tm": 0}, MESH)

    def step_into(src, dst, offset, snap, p, summed=False):
        for layer in (p, depth - 1 - p):
            flows = flow_at(flow, snap, layer)
            temper = temper_step(src, flows, layer)
            dst[A, layer + offset] = temper
            dst[B, layer + offset] = dopant_step(src, flows, layer)
            if summed:
                total[layer] = src[A, layer + 1] + temper

    @pl.when(first_phase)
    def _():
        send_halo(halo0[A])
        send_halo(halo0[B])

    load_snaps.wait()

    @pl.when(t == source)
    def _():
        for i in range(steps):
            pick_out[i] = jnp.full(pick_out.shape[1:], snaps[0, i].astype(jnp.float32))
        send_pick.start()
        for each in raws:
            each.start()

    clear_ends(x0, x1)
    pl.when(first_phase)(lambda: load_state.wait())
    load_flow.wait()

    @pl.when(t == 0)
    def _():
        raws[0].wait_recv()
        raws[1].wait_recv()
        send_halo(relay0)
        send_pick.wait_recv()
        raws[2].wait_recv()

        @pl.loop(0, pairs)
        def _(i):
            p = pairs - 1 - i

            @pl.when(p == 0)
            def _():
                recv_halo(relay0)

            for layer in (p, depth - 1 - p):
                x1[B, layer + 1] = dopant_step(x0, flow_picked(flow, pick[steps - 1], layer), layer)

        send_halo(halo1[B])

        @pl.loop(0, pairs)
        def _(i):
            p = pairs - 1 - i

            @pl.when(p == 0)
            def _():
                recv_halo(halo1[B])

            for layer in (p, depth - 1 - p):
                x2[B, layer] = dopant_step(x1, flow_picked(flow, pick[0], layer), layer)

        send_halo(halo2[B])
        for p in range(pairs):
            pass_pair(B, p, mate)

    @pl.when(first_phase)
    def _():
        @pl.loop(0, pairs)
        def _(i):
            p = pairs - 1 - i

            @pl.when(p == 0)
            def _():
                recv_halo(halo0[A])
                recv_halo(halo0[B])

            step_into(x0, x1, 1, snaps[0, steps - 1], p)

        send_halo(halo1[A])
        pl.when(t != source)(lambda: send_halo(halo1[B]))

        @pl.loop(0, pairs)
        def _(i):
            p = pairs - 1 - i

            @pl.when(p == 0)
            def _():
                recv_halo(halo1[A])
                pl.when(t != source)(lambda: recv_halo(halo1[B]))

            for layer in (p, depth - 1 - p):
                flows = flow_at(flow, snaps[0, 0], layer)
                temper = temper_step(x1, flows, layer)
                x2[A, layer] = temper
                total[layer] = x1[A, layer + 1] + temper

            @pl.when(t != source)
            def _():
                for layer in (p, depth - 1 - p):
                    x2[B, layer] = dopant_step(x1, flow_at(flow, snaps[0, 0], layer), layer)

            @pl.when(p == pairs - 1)
            def _():
                pass_pair(A, p, t - 1)

        send_halo(halo2[A])
        pl.when(t != source)(lambda: send_halo(halo2[B]))

        @pl.loop(0, pairs - 1)
        def _(p):
            pass_pair(A, p, t - 1)

        @pl.when(t != source)
        def _():
            @pl.loop(0, pairs)
            def _(p):
                pass_pair(B, p, mate)

    rows = total.shape[1] // slabs
    parts = ((1, depth - 2), (0, 1), (depth - 1, 1))
    inner, outer = (0,), (1, 2)

    class Share:
        def __init__(self, first, count, dst, slot, target):
            self.copies = [
                pltpu.make_async_remote_copy(
                    total.at[pl.ds(layer, layers), pl.ds(first * rows, count * rows)],
                    dst.at[pl.ds(layer, layers)], grad_send.at[target, part], grad_recv.at[slot, part],
                    {"tm": target}, MESH)
                for part, (layer, layers) in enumerate(parts)
            ]

        def start(self, which=inner + outer):
            for part in which:
                self.copies[part].start()

        def wait_recv(self):
            for copy in self.copies:
                copy.wait_recv()

        def wait_send(self):
            for copy in self.copies:
                copy.wait_send()

    mate0 = Share(1, 3, from_mate, 0, 1)
    mate3 = Share(0, 3, from_mate, 0, 2)
    back1 = Share(0, 1, from_late, 2, 0)
    back2 = Share(3, 1, from_late, 2, 3)
    cross20 = Share(0, 1, from_early, 1, 0)
    cross21 = Share(1, 1, from_early, 1, 1)
    cross12 = Share(2, 1, from_early, 1, 2)
    cross13 = Share(3, 1, from_early, 1, 3)

    def give(which):
        @pl.when(t == 0)
        def _():
            mate0.start(which)

        @pl.when(t == 1)
        def _():
            if which == inner:
                mate0.wait_recv()
            for layer, layers in (parts[part] for part in which):
                total[layer:layer + layers, rows:] += from_mate[layer:layer + layers]
            for each in (cross12, cross13, back1):
                each.start(which)

        @pl.when(t == 2)
        def _():
            if which == inner:
                mate3.wait_recv()
            for layer, layers in (parts[part] for part in which):
                total[layer:layer + layers, :3 * rows] += from_mate[layer:layer + layers]
            for each in (cross20, cross21, back2):
                each.start(which)

    pl.when(t == slabs - 1)(lambda: mate3.start())

    @pl.when(second_phase)
    def _():
        clear_ends(y0, y1)

        slow = t == source - 1

        for p in range(pairs):
            arrived(B, p, mate)

        arrived(A, 0, t + 1)

        @pl.when(jnp.logical_not(slow))
        def _():
            for p in range(1, pairs):
                arrived(A, p, t + 1)

        @pl.loop(0, pairs)
        def _(i):
            p = lax.rem(i + jnp.where(slow, 0, 1), pairs)

            @pl.when(jnp.logical_and(slow, i < pairs - 1))
            def _():
                arrived(A, i + 1, t + 1)

            @pl.when(p == 0)
            def _():
                recv_halo(halo2[A])
                recv_halo(halo2[B])

            step_into(y0, y1, 1, snaps[0, steps - 1], p)

            @pl.when(p == 0)
            def _():
                send_halo(halo3[A])
                send_halo(halo3[B])

        @pl.loop(0, pairs)
        def _(i):
            p = pairs - 1 - i

            @pl.when(p == 0)
            def _():
                give(inner)
                recv_halo(halo3[A])
                recv_halo(halo3[B])

            step_into(y1, y2, 0, snaps[0, 0], p, summed=True)

        give(outer)

    store_mid = pltpu.make_async_copy(y2, out, out_sem)
    store_end = pltpu.make_async_copy(x2, out, out_sem)
    pl.when(second_phase)(lambda: store_mid.start())
    pl.when(t == slabs - 1)(lambda: store_end.start())

    def mine(index):
        return total[:, index * rows:(index + 1) * rows]

    scale = 1.0 / steps

    @pl.when(t == 0)
    def _():
        cross20.wait_recv()
        back1.wait_recv()
        grad[...] = (mine(0) + from_late[...] + from_early[...]) * scale
        mate0.wait_send()

    @pl.when(t == 1)
    def _():
        cross21.wait_recv()
        grad[...] = (mine(1) + from_early[...]) * scale
        cross12.wait_send()
        cross13.wait_send()
        back1.wait_send()

    @pl.when(t == 2)
    def _():
        cross12.wait_recv()
        grad[...] = (mine(2) + from_early[...]) * scale
        cross20.wait_send()
        cross21.wait_send()
        back2.wait_send()

    @pl.when(t == 3)
    def _():
        back2.wait_recv()
        cross13.wait_recv()
        grad[...] = (mine(3) + from_late[...] + from_early[...]) * scale
        mate3.wait_send()

    @pl.when(t == 0)
    def _():
        sent_halo(relay0)

    @pl.when(t == source)
    def _():
        send_pick.wait_send()
        for each in raws:
            each.wait_send()

    @pl.when(first_phase)
    def _():
        for each in (halo0[A], halo0[B], halo1[A], halo2[A]):
            sent_halo(each)

        @pl.loop(0, depth)
        def _(layer):
            passing(A, layer, t - 1).wait_send()

    @pl.when(t != source)
    def _():
        sent_halo(halo1[B])
        sent_halo(halo2[B])

        @pl.loop(0, depth)
        def _(layer):
            passing(B, layer, mate).wait_send()

    @pl.when(second_phase)
    def _():
        sent_halo(halo3[A])
        sent_halo(halo3[B])
        store_mid.wait()

    pl.when(t == slabs - 1)(lambda: store_end.wait())


def body(slabs, blocks, slab_states, velocity, snap_of_step):
    state = slab_states[0]
    fields, depth, ny, nz = state.shape
    rows = ny // slabs
    f32 = jnp.float32
    widened = pltpu.VMEM((fields, depth + 2, ny, nz), f32)
    plain = pltpu.VMEM((fields, depth, ny, nz), f32)
    dma = pltpu.SemaphoreType.DMA
    final, gradient = pl.pallas_call(
        functools.partial(kernel, slabs, blocks),
        out_shape=(
            jax.ShapeDtypeStruct(state.shape, f32),
            jax.ShapeDtypeStruct((depth, rows, nz), f32),
        ),
        in_specs=[
            pl.BlockSpec(memory_space=pltpu.HBM),
            pl.BlockSpec(memory_space=pltpu.HBM),
            pl.BlockSpec(memory_space=pltpu.HBM),
        ],
        out_specs=(pl.BlockSpec(memory_space=pl.ANY), pl.BlockSpec(memory_space=pltpu.VMEM)),
        scratch_shapes=[
            widened, widened, plain, widened, widened, plain,
            pltpu.VMEM(velocity.shape, f32),
            pltpu.VMEM((depth, ny, nz), f32),
            pltpu.VMEM((depth, 3 * rows, nz), f32),
            pltpu.VMEM((depth, rows, nz), f32),
            pltpu.VMEM((depth, rows, nz), f32),
            pltpu.SMEM(snap_of_step.shape, jnp.int32),
            pltpu.VMEM((snap_of_step.shape[1], 8, 128), f32),
            pltpu.VMEM((snap_of_step.shape[1], 8, 128), f32),
            dma((3,)), dma((4, 2, 2)), dma((4, 2, 2)), dma((fields, depth)), dma((fields, depth)), dma((4,)), dma((4,)),
            dma((slabs, 3)), dma((3, 3)), dma,
        ],
        compiler_params=pltpu.CompilerParams(
            collective_id=0, has_side_effects=True, vmem_limit_bytes=32 * 1024 * 1024),
        cost_estimate=pl.CostEstimate(flops=200 * state.size, bytes_accessed=28 * state.size, transcendentals=0),
    )(*(pltpu.with_memory_space_constraint(x, pltpu.HBM) for x in (state, velocity, snap_of_step)))
    return final[None], gradient


def solution(mesh):
    placed = (P("tm", None, "space", None, None), P(None, None, "space", None, None), P("tm", None))
    return jax.shard_map(
        functools.partial(body, mesh.shape["tm"], mesh.shape["space"]),
        mesh=mesh,
        in_specs=placed,
        out_specs=(P("tm", None, "space", None, None), P("space", "tm", None)),
        check_vma=False,
    )
```

```python
import functools

import jax
import jax.numpy as jnp
from jax import lax
from jax.experimental import pallas as pl
from jax.experimental.pallas import tpu as pltpu
from jax.sharding import PartitionSpec as P

coupling = 0.3
MESH = pl.DeviceIdType.MESH


def shifted(field):
    rows, lanes = field.shape
    row = lax.broadcasted_iota(jnp.int32, field.shape, 0)
    lane = lax.broadcasted_iota(jnp.int32, field.shape, 1)
    north = jnp.where(row == rows - 1, 0.0, pltpu.roll(field, rows - 1, 0))
    south = jnp.where(row == 0, 0.0, pltpu.roll(field, 1, 0))
    upper = jnp.where(lane == lanes - 1, 0.0, pltpu.roll(field, lanes - 1, 1))
    lower = jnp.where(lane == 0, 0.0, pltpu.roll(field, 1, 1))
    return north, south, upper, lower


def moved(west, centre, east, u, v, w, rate):
    north, south, upper, lower = shifted(centre)
    around = (east + west) + (north + south) + (upper + lower)
    transport = u * (east - west) + v * (north - south) + w * (upper - lower)
    return (1.0 - 6.0 * rate) * centre + rate * around + 0.25 * transport


def flow_at(flow, snap, layer):
    return tuple(flow[snap, c, layer] for c in range(3))


def flow_picked(flow, pick, layer):
    rows, lanes = flow.shape[3:]
    pick = jnp.concatenate([pick] * (lanes // pick.shape[1]), axis=1)
    pick = jnp.concatenate([pick] * (rows // pick.shape[0]), axis=0)
    return tuple(jnp.where(pick > 0.5, flow[1, c, layer], flow[0, c, layer]) for c in range(3))


def temper_step(src, flows, layer):
    a, b = src[0, layer + 1], src[1, layer + 1]
    return moved(src[0, layer], a, src[0, layer + 2], *flows, 0.14) + coupling * b


def dopant_step(src, flows, layer):
    return moved(src[1, layer], src[1, layer + 1], src[1, layer + 2], *flows, 0.06)


def kernel(
    slabs, blocks, state, velocity, snaps_in, out, grad,
    x0, x1, x2, y0, y1, y2, flow, total, from_mate, from_early, from_late, snaps, pick_out, pick,
    load_sem, halo_send, halo_recv, pass_send, pass_recv, raw_send, raw_recv, grad_send, grad_recv, out_sem,
):
    t, s = lax.axis_index("tm"), lax.axis_index("space")
    depth = x2.shape[1]
    pairs = depth // 2
    steps = snaps.shape[1]
    has_up, has_down = s < blocks - 1, s > 0
    first_phase, second_phase = t > 0, t < slabs - 1
    mate = t + 1 - 2 * lax.rem(t, 2)
    source = slabs // 2

    load_state = pltpu.make_async_copy(state, x0.at[:, pl.ds(1, depth)], load_sem.at[0])
    load_flow = pltpu.make_async_copy(velocity, flow, load_sem.at[1])
    load_snaps = pltpu.make_async_copy(snaps_in, snaps, load_sem.at[2])

    load_snaps.start()

    @pl.when(first_phase)
    def _():
        load_state.start()

    load_flow.start()

    barrier = pltpu.get_barrier_semaphore()

    def greet(target):
        pl.semaphore_signal(barrier, inc=1, device_id=target, device_id_type=MESH)

    for other in range(1, slabs):
        greet({"tm": lax.rem(t + other, slabs)})
    for by, there in ((1, has_up), (-1, has_down)):
        @pl.when(there)
        def _(by=by):
            greet({"space": s + by})
            pl.when(first_phase)(lambda: greet({"tm": t - 1, "space": s + by}))
            pl.when(second_phase)(lambda: greet({"tm": t + 1, "space": s + by}))

    sides = jnp.where(has_up, 1, 0) + jnp.where(has_down, 1, 0)
    rounds = 1 + jnp.where(first_phase, 1, 0) + jnp.where(second_phase, 1, 0)
    pl.semaphore_wait(barrier, slabs - 1 + sides * rounds)

    def halo(k, field, low, high, buf, tm=t):
        def copy(source, layer, side, by):
            return pltpu.make_async_remote_copy(
                source, buf.at[field, layer], halo_send.at[k, field, side], halo_recv.at[k, field, side],
                {"tm": tm, "space": s + by}, MESH)

        return copy(high, 0, 0, 1), copy(low, depth + 1, 1, -1)

    def send_halo(pair):
        pl.when(has_up)(lambda: pair[0].start())
        pl.when(has_down)(lambda: pair[1].start())

    def recv_halo(pair):
        pl.when(has_down)(lambda: pair[0].wait_recv())
        pl.when(has_up)(lambda: pair[1].wait_recv())

    def sent_halo(pair):
        pl.when(has_up)(lambda: pair[0].wait_send())
        pl.when(has_down)(lambda: pair[1].wait_send())

    def clear_ends(*bufs):
        for buf in bufs:
            @pl.when(s == 0)
            def _(buf=buf):
                buf[:, 0] = jnp.zeros(buf.shape[:1] + buf.shape[2:], jnp.float32)

            @pl.when(s == blocks - 1)
            def _(buf=buf):
                buf[:, depth + 1] = jnp.zeros(buf.shape[:1] + buf.shape[2:], jnp.float32)

    A, B = 0, 1
    halo0 = [halo(0, f, state.at[f, 0], state.at[f, depth - 1], x0) for f in (A, B)]
    relay0 = halo(0, B, x0.at[B, 1], x0.at[B, depth], x0)
    halo1 = [halo(1, f, x1.at[f, 1], x1.at[f, depth], x1) for f in (A, B)]
    halo2 = [halo(2, f, x2.at[f, 0], x2.at[f, depth - 1], y0, (t - 1, mate)[f]) for f in (A, B)]
    halo3 = [halo(3, f, y1.at[f, 1], y1.at[f, depth], y1) for f in (A, B)]

    def passing(field, layer, target):
        return pltpu.make_async_remote_copy(
            x2.at[field, layer], y0.at[field, layer + 1], pass_send.at[field, layer], pass_recv.at[field, layer],
            {"tm": target}, MESH)

    def pass_pair(field, p, target):
        passing(field, p, target).start()
        passing(field, depth - 1 - p, target).start()

    def arrived(field, p, origin):
        passing(field, p, origin).wait_recv()
        passing(field, depth - 1 - p, origin).wait_recv()

    def raw(part, layer, layers):
        return pltpu.make_async_remote_copy(
            state.at[B, pl.ds(layer, layers)], x0.at[B, pl.ds(layer + 1, layers)],
            raw_send.at[part], raw_recv.at[part], {"tm": 0}, MESH)

    raws = [raw(0, 0, 1), raw(1, depth - 1, 1), raw(2, 1, depth - 2)]
    send_pick = pltpu.make_async_remote_copy(pick_out, pick, raw_send.at[3], raw_recv.at[3], {"tm": 0}, MESH)

    def step_into(src, dst, offset, snap, p, summed=False):
        for layer in (p, depth - 1 - p):
            flows = flow_at(flow, snap, layer)
            temper = temper_step(src, flows, layer)
            dst[A, layer + offset] = temper
            dst[B, layer + offset] = dopant_step(src, flows, layer)
            if summed:
                total[layer] = src[A, layer + 1] + temper

    @pl.when(first_phase)
    def _():
        send_halo(halo0[A])
        send_halo(halo0[B])

    load_snaps.wait()

    @pl.when(t == source)
    def _():
        for i in range(steps):
            pick_out[i] = jnp.full(pick_out.shape[1:], snaps[0, i].astype(jnp.float32))
        send_pick.start()
        for each in raws:
            each.start()

    clear_ends(x0, x1)
    pl.when(first_phase)(lambda: load_state.wait())
    load_flow.wait()

    @pl.when(t == 0)
    def _():
        raws[0].wait_recv()
        raws[1].wait_recv()
        send_halo(relay0)
        send_pick.wait_recv()
        raws[2].wait_recv()

        @pl.loop(0, pairs)
        def _(i):
            p = pairs - 1 - i

            @pl.when(p == 0)
            def _():
                recv_halo(relay0)

            for layer in (p, depth - 1 - p):
                x1[B, layer + 1] = dopant_step(x0, flow_picked(flow, pick[steps - 1], layer), layer)

        send_halo(halo1[B])

        @pl.loop(0, pairs)
        def _(i):
            p = pairs - 1 - i

            @pl.when(p == 0)
            def _():
                recv_halo(halo1[B])

            for layer in (p, depth - 1 - p):
                x2[B, layer] = dopant_step(x1, flow_picked(flow, pick[0], layer), layer)

        send_halo(halo2[B])
        for p in range(pairs):
            pass_pair(B, p, mate)

    @pl.when(first_phase)
    def _():
        @pl.loop(0, pairs)
        def _(i):
            p = pairs - 1 - i

            @pl.when(p == 0)
            def _():
                recv_halo(halo0[A])
                recv_halo(halo0[B])

            step_into(x0, x1, 1, snaps[0, steps - 1], p)

        send_halo(halo1[A])
        pl.when(t != source)(lambda: send_halo(halo1[B]))

        @pl.loop(0, pairs)
        def _(i):
            p = pairs - 1 - i

            @pl.when(p == 0)
            def _():
                recv_halo(halo1[A])
                pl.when(t != source)(lambda: recv_halo(halo1[B]))

            for layer in (p, depth - 1 - p):
                flows = flow_at(flow, snaps[0, 0], layer)
                temper = temper_step(x1, flows, layer)
                x2[A, layer] = temper
                total[layer] = x1[A, layer + 1] + temper

            @pl.when(t != source)
            def _():
                for layer in (p, depth - 1 - p):
                    x2[B, layer] = dopant_step(x1, flow_at(flow, snaps[0, 0], layer), layer)

            @pl.when(p > 0)
            def _():
                pass_pair(A, p, t - 1)
                pl.when(t != source)(lambda: pass_pair(B, p, mate))

        send_halo(halo2[A])
        pl.when(t != source)(lambda: send_halo(halo2[B]))
        pass_pair(A, 0, t - 1)
        pl.when(t != source)(lambda: pass_pair(B, 0, mate))

    rows = total.shape[1] // slabs
    parts = ((1, depth - 2), (0, 1), (depth - 1, 1))
    inner, outer = (0,), (1, 2)

    class Share:
        def __init__(self, first, count, dst, slot, target):
            self.copies = [
                pltpu.make_async_remote_copy(
                    total.at[pl.ds(layer, layers), pl.ds(first * rows, count * rows)],
                    dst.at[pl.ds(layer, layers)], grad_send.at[target, part], grad_recv.at[slot, part],
                    {"tm": target}, MESH)
                for part, (layer, layers) in enumerate(parts)
            ]

        def start(self, which=inner + outer):
            for part in which:
                self.copies[part].start()

        def wait_recv(self):
            for copy in self.copies:
                copy.wait_recv()

        def wait_send(self):
            for copy in self.copies:
                copy.wait_send()

    mate0 = Share(1, 3, from_mate, 0, 1)
    mate3 = Share(0, 3, from_mate, 0, 2)
    back1 = Share(0, 1, from_late, 2, 0)
    back2 = Share(3, 1, from_late, 2, 3)
    cross20 = Share(0, 1, from_early, 1, 0)
    cross21 = Share(1, 1, from_early, 1, 1)
    cross12 = Share(2, 1, from_early, 1, 2)
    cross13 = Share(3, 1, from_early, 1, 3)

    def give(which):
        @pl.when(t == 0)
        def _():
            mate0.start(which)

        @pl.when(t == 1)
        def _():
            if which == inner:
                mate0.wait_recv()
            for layer, layers in (parts[part] for part in which):
                total[layer:layer + layers, rows:] += from_mate[layer:layer + layers]
            for each in (cross12, cross13, back1):
                each.start(which)

        @pl.when(t == 2)
        def _():
            if which == inner:
                mate3.wait_recv()
            for layer, layers in (parts[part] for part in which):
                total[layer:layer + layers, :3 * rows] += from_mate[layer:layer + layers]
            for each in (cross20, cross21, back2):
                each.start(which)

    pl.when(t == slabs - 1)(lambda: mate3.start())

    @pl.when(second_phase)
    def _():
        clear_ends(y0, y1)

        def ready(p):
            arrived(B, p, mate)
            arrived(A, p, t + 1)

        ready(pairs - 1)

        @pl.loop(0, pairs)
        def _(i):
            p = jnp.where(i < pairs - 2, pairs - 1 - i, i - (pairs - 2))
            pl.when(i < pairs - 1)(lambda: ready(pairs - 2 - i))

            @pl.when(p == 0)
            def _():
                recv_halo(halo2[A])
                recv_halo(halo2[B])

            step_into(y0, y1, 1, snaps[0, steps - 1], p)

            @pl.when(p == 0)
            def _():
                send_halo(halo3[A])
                send_halo(halo3[B])

        @pl.loop(0, pairs)
        def _(i):
            p = pairs - 1 - i

            @pl.when(p == 0)
            def _():
                give(inner)
                recv_halo(halo3[A])
                recv_halo(halo3[B])

            step_into(y1, y2, 0, snaps[0, 0], p, summed=True)

        give(outer)

    store_mid = pltpu.make_async_copy(y2, out, out_sem)
    store_end = pltpu.make_async_copy(x2, out, out_sem)
    pl.when(second_phase)(lambda: store_mid.start())
    pl.when(t == slabs - 1)(lambda: store_end.start())

    def mine(index):
        return total[:, index * rows:(index + 1) * rows]

    scale = 1.0 / steps

    @pl.when(t == 0)
    def _():
        cross20.wait_recv()
        back1.wait_recv()
        grad[...] = (mine(0) + from_late[...] + from_early[...]) * scale
        mate0.wait_send()

    @pl.when(t == 1)
    def _():
        cross21.wait_recv()
        grad[...] = (mine(1) + from_early[...]) * scale
        cross12.wait_send()
        cross13.wait_send()
        back1.wait_send()

    @pl.when(t == 2)
    def _():
        cross12.wait_recv()
        grad[...] = (mine(2) + from_early[...]) * scale
        cross20.wait_send()
        cross21.wait_send()
        back2.wait_send()

    @pl.when(t == 3)
    def _():
        back2.wait_recv()
        cross13.wait_recv()
        grad[...] = (mine(3) + from_late[...] + from_early[...]) * scale
        mate3.wait_send()

    @pl.when(t == 0)
    def _():
        sent_halo(relay0)

    @pl.when(t == source)
    def _():
        send_pick.wait_send()
        for each in raws:
            each.wait_send()

    @pl.when(first_phase)
    def _():
        for each in (halo0[A], halo0[B], halo1[A], halo2[A]):
            sent_halo(each)

        @pl.loop(0, depth)
        def _(layer):
            passing(A, layer, t - 1).wait_send()

    @pl.when(t != source)
    def _():
        sent_halo(halo1[B])
        sent_halo(halo2[B])

        @pl.loop(0, depth)
        def _(layer):
            passing(B, layer, mate).wait_send()

    @pl.when(second_phase)
    def _():
        sent_halo(halo3[A])
        sent_halo(halo3[B])
        store_mid.wait()

    pl.when(t == slabs - 1)(lambda: store_end.wait())


def write_kernel(final, grad, final_out, grad_out, sems):
    copies = [pltpu.make_async_copy(final, final_out, sems.at[0]), pltpu.make_async_copy(grad, grad_out, sems.at[1])]
    for each in copies:
        each.start()
    for each in copies:
        each.wait()


def written(final, gradient):
    return pl.pallas_call(
        write_kernel,
        out_shape=[jax.ShapeDtypeStruct(x.shape, x.dtype) for x in (final, gradient)],
        in_specs=[pl.BlockSpec(memory_space=pl.ANY)] * 2,
        out_specs=[pl.BlockSpec(memory_space=pl.ANY)] * 2,
        scratch_shapes=[pltpu.SemaphoreType.DMA((2,))],
    )(final, gradient)


def body(slabs, blocks, slab_states, velocity, snap_of_step):
    state = slab_states[0]
    fields, depth, ny, nz = state.shape
    rows = ny // slabs
    f32 = jnp.float32
    widened = pltpu.VMEM((fields, depth + 2, ny, nz), f32)
    plain = pltpu.VMEM((fields, depth, ny, nz), f32)
    dma = pltpu.SemaphoreType.DMA
    final, gradient = pl.pallas_call(
        functools.partial(kernel, slabs, blocks),
        out_shape=(
            jax.ShapeDtypeStruct(state.shape, f32),
            jax.ShapeDtypeStruct((depth, rows, nz), f32),
        ),
        in_specs=[
            pl.BlockSpec(memory_space=pltpu.HBM),
            pl.BlockSpec(memory_space=pltpu.HBM),
            pl.BlockSpec(memory_space=pltpu.HBM),
        ],
        out_specs=(pl.BlockSpec(memory_space=pl.ANY), pl.BlockSpec(memory_space=pltpu.VMEM)),
        scratch_shapes=[
            widened, widened, plain, widened, widened, plain,
            pltpu.VMEM(velocity.shape, f32),
            pltpu.VMEM((depth, ny, nz), f32),
            pltpu.VMEM((depth, 3 * rows, nz), f32),
            pltpu.VMEM((depth, rows, nz), f32),
            pltpu.VMEM((depth, rows, nz), f32),
            pltpu.SMEM(snap_of_step.shape, jnp.int32),
            pltpu.VMEM((snap_of_step.shape[1], 8, 128), f32),
            pltpu.VMEM((snap_of_step.shape[1], 8, 128), f32),
            dma((3,)), dma((4, 2, 2)), dma((4, 2, 2)), dma((fields, depth)), dma((fields, depth)), dma((4,)), dma((4,)),
            dma((slabs, 3)), dma((3, 3)), dma,
        ],
        compiler_params=pltpu.CompilerParams(
            collective_id=0, has_side_effects=True, vmem_limit_bytes=32 * 1024 * 1024),
        cost_estimate=pl.CostEstimate(flops=200 * state.size, bytes_accessed=28 * state.size, transcendentals=0),
    )(*(pltpu.with_memory_space_constraint(x, pltpu.HBM) for x in (state, velocity, snap_of_step)))
    final, gradient = written(final, gradient)
    return final[None], gradient


def solution(mesh):
    placed = (P("tm", None, "space", None, None), P(None, None, "space", None, None), P("tm", None))
    return jax.shard_map(
        functools.partial(body, mesh.shape["tm"], mesh.shape["space"]),
        mesh=mesh,
        in_specs=placed,
        out_specs=(P("tm", None, "space", None, None), P("space", "tm", None)),
        check_vma=False,
    )
```

```python
import functools

import jax
import jax.numpy as jnp
from jax import lax
from jax.experimental import pallas as pl
from jax.experimental.pallas import tpu as pltpu
from jax.sharding import PartitionSpec as P

coupling = 0.3
MESH = pl.DeviceIdType.MESH


def shifted(field):
    rows, lanes = field.shape
    row = lax.broadcasted_iota(jnp.int32, (8, lanes), 0)
    lane = lax.broadcasted_iota(jnp.int32, (rows, 128), 1)
    north = pltpu.roll(field, rows - 1, 0)
    north = jnp.concatenate([north[:-8], jnp.where(row == 7, 0.0, north[-8:])], axis=0)
    south = pltpu.roll(field, 1, 0)
    south = jnp.concatenate([jnp.where(row == 0, 0.0, south[:8]), south[8:]], axis=0)
    upper = pltpu.roll(field, lanes - 1, 1)
    upper = jnp.concatenate([upper[:, :-128], jnp.where(lane == 127, 0.0, upper[:, -128:])], axis=1)
    lower = pltpu.roll(field, 1, 1)
    lower = jnp.concatenate([jnp.where(lane == 0, 0.0, lower[:, :128]), lower[:, 128:]], axis=1)
    return north, south, upper, lower


def moved(west, centre, east, u, v, w, rate):
    north, south, upper, lower = shifted(centre)
    around = (east + west) + (north + south) + (upper + lower)
    transport = u * (east - west) + v * (north - south) + w * (upper - lower)
    return (1.0 - 6.0 * rate) * centre + rate * around + 0.25 * transport


def flow_at(flow, snap, layer):
    return tuple(flow[snap, c, layer] for c in range(3))


def flow_picked(flow, pick, layer):
    rows, lanes = flow.shape[3:]
    pick = jnp.concatenate([pick] * (lanes // pick.shape[1]), axis=1)
    pick = jnp.concatenate([pick] * (rows // pick.shape[0]), axis=0)
    return tuple(jnp.where(pick > 0.5, flow[1, c, layer], flow[0, c, layer]) for c in range(3))


def temper_step(src, flows, layer):
    a, b = src[0, layer + 1], src[1, layer + 1]
    return moved(src[0, layer], a, src[0, layer + 2], *flows, 0.14) + coupling * b


def dopant_step(src, flows, layer):
    return moved(src[1, layer], src[1, layer + 1], src[1, layer + 2], *flows, 0.06)


def kernel(
    slabs, blocks, state, velocity, snaps_in, out, grad,
    x0, x1, x2, y0, y1, y2, flow, total, from_mate, from_early, from_late, snaps, pick_out, pick,
    load_sem, halo_send, halo_recv, pass_send, pass_recv, raw_send, raw_recv, grad_send, grad_recv, out_sem,
):
    t, s = lax.axis_index("tm"), lax.axis_index("space")
    depth = x2.shape[1]
    pairs = depth // 2
    steps = snaps.shape[1]
    has_up, has_down = s < blocks - 1, s > 0
    first_phase, second_phase = t > 0, t < slabs - 1
    mate = t + 1 - 2 * lax.rem(t, 2)
    source = slabs // 2

    load_state = pltpu.make_async_copy(state, x0.at[:, pl.ds(1, depth)], load_sem.at[0])
    load_flow = pltpu.make_async_copy(velocity, flow, load_sem.at[1])
    load_snaps = pltpu.make_async_copy(snaps_in, snaps, load_sem.at[2])

    load_snaps.start()

    @pl.when(first_phase)
    def _():
        load_state.start()

    load_flow.start()

    barrier = pltpu.get_barrier_semaphore()

    def greet(target):
        pl.semaphore_signal(barrier, inc=1, device_id=target, device_id_type=MESH)

    for other in range(1, slabs):
        greet({"tm": lax.rem(t + other, slabs)})
    for by, there in ((1, has_up), (-1, has_down)):
        @pl.when(there)
        def _(by=by):
            greet({"space": s + by})
            pl.when(first_phase)(lambda: greet({"tm": t - 1, "space": s + by}))
            pl.when(second_phase)(lambda: greet({"tm": t + 1, "space": s + by}))

    sides = jnp.where(has_up, 1, 0) + jnp.where(has_down, 1, 0)
    rounds = 1 + jnp.where(first_phase, 1, 0) + jnp.where(second_phase, 1, 0)
    pl.semaphore_wait(barrier, slabs - 1 + sides * rounds)

    def halo(k, field, low, high, buf, tm=t):
        def copy(source, layer, side, by):
            return pltpu.make_async_remote_copy(
                source, buf.at[field, layer], halo_send.at[k, field, side], halo_recv.at[k, field, side],
                {"tm": tm, "space": s + by}, MESH)

        return copy(high, 0, 0, 1), copy(low, depth + 1, 1, -1)

    def send_halo(pair):
        pl.when(has_up)(lambda: pair[0].start())
        pl.when(has_down)(lambda: pair[1].start())

    def recv_halo(pair):
        pl.when(has_down)(lambda: pair[0].wait_recv())
        pl.when(has_up)(lambda: pair[1].wait_recv())

    def sent_halo(pair):
        pl.when(has_up)(lambda: pair[0].wait_send())
        pl.when(has_down)(lambda: pair[1].wait_send())

    def clear_ends(*bufs):
        for buf in bufs:
            @pl.when(s == 0)
            def _(buf=buf):
                buf[:, 0] = jnp.zeros(buf.shape[:1] + buf.shape[2:], jnp.float32)

            @pl.when(s == blocks - 1)
            def _(buf=buf):
                buf[:, depth + 1] = jnp.zeros(buf.shape[:1] + buf.shape[2:], jnp.float32)

    A, B = 0, 1
    halo0 = [halo(0, f, state.at[f, 0], state.at[f, depth - 1], x0) for f in (A, B)]
    relay0 = halo(0, B, x0.at[B, 1], x0.at[B, depth], x0)
    halo1 = [halo(1, f, x1.at[f, 1], x1.at[f, depth], x1) for f in (A, B)]
    halo2 = [halo(2, f, x2.at[f, 0], x2.at[f, depth - 1], y0, (t - 1, mate)[f]) for f in (A, B)]
    halo3 = [halo(3, f, y1.at[f, 1], y1.at[f, depth], y1) for f in (A, B)]

    def passing(field, layer, target):
        return pltpu.make_async_remote_copy(
            x2.at[field, layer], y0.at[field, layer + 1], pass_send.at[field, layer], pass_recv.at[field, layer],
            {"tm": target}, MESH)

    def pass_pair(field, p, target):
        passing(field, p, target).start()
        passing(field, depth - 1 - p, target).start()

    def arrived(field, p, origin):
        passing(field, p, origin).wait_recv()
        passing(field, depth - 1 - p, origin).wait_recv()

    def raw(part, layer, layers):
        return pltpu.make_async_remote_copy(
            state.at[B, pl.ds(layer, layers)], x0.at[B, pl.ds(layer + 1, layers)],
            raw_send.at[part], raw_recv.at[part], {"tm": 0}, MESH)

    raws = [raw(0, 0, 1), raw(1, depth - 1, 1), raw(2, 1, depth - 2)]
    send_pick = pltpu.make_async_remote_copy(pick_out, pick, raw_send.at[3], raw_recv.at[3], {"tm": 0}, MESH)

    def step_into(src, dst, offset, snap, p, summed=False):
        for layer in (p, depth - 1 - p):
            flows = flow_at(flow, snap, layer)
            temper = temper_step(src, flows, layer)
            dst[A, layer + offset] = temper
            dst[B, layer + offset] = dopant_step(src, flows, layer)
            if summed:
                total[layer] = src[A, layer + 1] + temper

    @pl.when(first_phase)
    def _():
        send_halo(halo0[A])
        send_halo(halo0[B])

    load_snaps.wait()

    @pl.when(t == source)
    def _():
        for i in range(steps):
            pick_out[i] = jnp.full(pick_out.shape[1:], snaps[0, i].astype(jnp.float32))
        send_pick.start()
        for each in raws:
            each.start()

    clear_ends(x0, x1)
    pl.when(first_phase)(lambda: load_state.wait())
    load_flow.wait()

    @pl.when(t == 0)
    def _():
        raws[0].wait_recv()
        raws[1].wait_recv()
        send_halo(relay0)
        send_pick.wait_recv()
        raws[2].wait_recv()

        @pl.loop(0, pairs)
        def _(i):
            p = pairs - 1 - i

            @pl.when(p == 0)
            def _():
                recv_halo(relay0)

            for layer in (p, depth - 1 - p):
                x1[B, layer + 1] = dopant_step(x0, flow_picked(flow, pick[steps - 1], layer), layer)

        send_halo(halo1[B])

        @pl.loop(0, pairs)
        def _(i):
            p = pairs - 1 - i

            @pl.when(p == 0)
            def _():
                recv_halo(halo1[B])

            for layer in (p, depth - 1 - p):
                x2[B, layer] = dopant_step(x1, flow_picked(flow, pick[0], layer), layer)

        send_halo(halo2[B])
        for p in range(pairs):
            pass_pair(B, p, mate)

    @pl.when(first_phase)
    def _():
        @pl.loop(0, pairs)
        def _(i):
            p = pairs - 1 - i

            @pl.when(p == 0)
            def _():
                recv_halo(halo0[A])
                recv_halo(halo0[B])

            step_into(x0, x1, 1, snaps[0, steps - 1], p)

        send_halo(halo1[A])
        pl.when(t != source)(lambda: send_halo(halo1[B]))

        @pl.loop(0, pairs)
        def _(i):
            p = pairs - 1 - i

            @pl.when(p == 0)
            def _():
                recv_halo(halo1[A])
                pl.when(t != source)(lambda: recv_halo(halo1[B]))

            for layer in (p, depth - 1 - p):
                flows = flow_at(flow, snaps[0, 0], layer)
                temper = temper_step(x1, flows, layer)
                x2[A, layer] = temper
                total[layer] = x1[A, layer + 1] + temper

            @pl.when(t != source)
            def _():
                for layer in (p, depth - 1 - p):
                    x2[B, layer] = dopant_step(x1, flow_at(flow, snaps[0, 0], layer), layer)

            @pl.when(p > 0)
            def _():
                pass_pair(A, p, t - 1)
                pl.when(t != source)(lambda: pass_pair(B, p, mate))

        send_halo(halo2[A])
        pl.when(t != source)(lambda: send_halo(halo2[B]))
        pass_pair(A, 0, t - 1)
        pl.when(t != source)(lambda: pass_pair(B, 0, mate))

    rows = total.shape[1] // slabs
    parts = ((2, depth - 4), (1, 1), (depth - 2, 1), (0, 1), (depth - 1, 1))
    inner, second, outer = (0,), (1, 2), (3, 4)

    class Share:
        def __init__(self, first, count, dst, slot, target):
            self.copies = [
                pltpu.make_async_remote_copy(
                    total.at[pl.ds(layer, layers), pl.ds(first * rows, count * rows)],
                    dst.at[pl.ds(layer, layers)], grad_send.at[target, part], grad_recv.at[slot, part],
                    {"tm": target}, MESH)
                for part, (layer, layers) in enumerate(parts)
            ]

        def start(self, which=inner + second + outer):
            for part in which:
                self.copies[part].start()

        def wait_recv(self):
            for copy in self.copies:
                copy.wait_recv()

        def wait_send(self):
            for copy in self.copies:
                copy.wait_send()

    mate0 = Share(1, 3, from_mate, 0, 1)
    mate3 = Share(0, 3, from_mate, 0, 2)
    back1 = Share(0, 1, from_late, 2, 0)
    back2 = Share(3, 1, from_late, 2, 3)
    cross20 = Share(0, 1, from_early, 1, 0)
    cross21 = Share(1, 1, from_early, 1, 1)
    cross12 = Share(2, 1, from_early, 1, 2)
    cross13 = Share(3, 1, from_early, 1, 3)

    def give(which):
        @pl.when(t == 0)
        def _():
            mate0.start(which)

        @pl.when(t == 1)
        def _():
            if which == inner:
                mate0.wait_recv()
            for layer, layers in (parts[part] for part in which):
                total[layer:layer + layers, rows:] += from_mate[layer:layer + layers]
            for each in (cross12, cross13, back1):
                each.start(which)

        @pl.when(t == 2)
        def _():
            if which == inner:
                mate3.wait_recv()
            for layer, layers in (parts[part] for part in which):
                total[layer:layer + layers, :3 * rows] += from_mate[layer:layer + layers]
            for each in (cross20, cross21, back2):
                each.start(which)

    pl.when(t == slabs - 1)(lambda: mate3.start())

    @pl.when(second_phase)
    def _():
        clear_ends(y0, y1)

        def ready(p):
            arrived(B, p, mate)
            arrived(A, p, t + 1)

        ready(pairs - 1)

        @pl.loop(0, pairs)
        def _(i):
            p = jnp.where(i < pairs - 2, pairs - 1 - i, i - (pairs - 2))
            pl.when(i < pairs - 1)(lambda: ready(pairs - 2 - i))

            @pl.when(p == 0)
            def _():
                recv_halo(halo2[A])
                recv_halo(halo2[B])

            step_into(y0, y1, 1, snaps[0, steps - 1], p)

            @pl.when(p == 0)
            def _():
                send_halo(halo3[A])
                send_halo(halo3[B])

        @pl.loop(0, pairs)
        def _(i):
            p = pairs - 1 - i

            @pl.when(p == 0)
            def _():
                recv_halo(halo3[A])
                recv_halo(halo3[B])

            step_into(y1, y2, 0, snaps[0, 0], p, summed=True)
            pl.when(p == 2)(lambda: give(inner))
            pl.when(p == 1)(lambda: give(second))

        give(outer)

    store_mid = pltpu.make_async_copy(y2, out, out_sem)
    store_end = pltpu.make_async_copy(x2, out, out_sem)
    pl.when(second_phase)(lambda: store_mid.start())
    pl.when(t == slabs - 1)(lambda: store_end.start())

    def mine(index):
        return total[:, index * rows:(index + 1) * rows]

    scale = 1.0 / steps

    @pl.when(t == 0)
    def _():
        cross20.wait_recv()
        back1.wait_recv()
        grad[...] = (mine(0) + from_late[...] + from_early[...]) * scale
        mate0.wait_send()

    @pl.when(t == 1)
    def _():
        cross21.wait_recv()
        grad[...] = (mine(1) + from_early[...]) * scale
        cross12.wait_send()
        cross13.wait_send()
        back1.wait_send()

    @pl.when(t == 2)
    def _():
        cross12.wait_recv()
        grad[...] = (mine(2) + from_early[...]) * scale
        cross20.wait_send()
        cross21.wait_send()
        back2.wait_send()

    @pl.when(t == 3)
    def _():
        back2.wait_recv()
        cross13.wait_recv()
        grad[...] = (mine(3) + from_late[...] + from_early[...]) * scale
        mate3.wait_send()

    @pl.when(t == 0)
    def _():
        sent_halo(relay0)

    @pl.when(t == source)
    def _():
        send_pick.wait_send()
        for each in raws:
            each.wait_send()

    @pl.when(first_phase)
    def _():
        for each in (halo0[A], halo0[B], halo1[A], halo2[A]):
            sent_halo(each)

        @pl.loop(0, depth)
        def _(layer):
            passing(A, layer, t - 1).wait_send()

    @pl.when(t != source)
    def _():
        sent_halo(halo1[B])
        sent_halo(halo2[B])

        @pl.loop(0, depth)
        def _(layer):
            passing(B, layer, mate).wait_send()

    @pl.when(second_phase)
    def _():
        sent_halo(halo3[A])
        sent_halo(halo3[B])
        store_mid.wait()

    pl.when(t == slabs - 1)(lambda: store_end.wait())


def write_kernel(final, grad, final_out, grad_out, sems):
    copies = [pltpu.make_async_copy(final, final_out, sems.at[0]), pltpu.make_async_copy(grad, grad_out, sems.at[1])]
    for each in copies:
        each.start()
    for each in copies:
        each.wait()


def written(final, gradient):
    return pl.pallas_call(
        write_kernel,
        out_shape=[jax.ShapeDtypeStruct(x.shape, x.dtype) for x in (final, gradient)],
        in_specs=[pl.BlockSpec(memory_space=pltpu.VMEM)] * 2,
        out_specs=[pl.BlockSpec(memory_space=pl.ANY)] * 2,
        scratch_shapes=[pltpu.SemaphoreType.DMA((2,))],
    )(*(pltpu.with_memory_space_constraint(x, pltpu.VMEM) for x in (final, gradient)))


def body(slabs, blocks, slab_states, velocity, snap_of_step):
    state = slab_states[0]
    fields, depth, ny, nz = state.shape
    rows = ny // slabs
    f32 = jnp.float32
    widened = pltpu.VMEM((fields, depth + 2, ny, nz), f32)
    plain = pltpu.VMEM((fields, depth, ny, nz), f32)
    dma = pltpu.SemaphoreType.DMA
    final, gradient = pl.pallas_call(
        functools.partial(kernel, slabs, blocks),
        out_shape=(
            jax.ShapeDtypeStruct(state.shape, f32),
            jax.ShapeDtypeStruct((depth, rows, nz), f32),
        ),
        in_specs=[
            pl.BlockSpec(memory_space=pltpu.HBM),
            pl.BlockSpec(memory_space=pltpu.HBM),
            pl.BlockSpec(memory_space=pltpu.HBM),
        ],
        out_specs=(pl.BlockSpec(memory_space=pl.ANY), pl.BlockSpec(memory_space=pltpu.VMEM)),
        scratch_shapes=[
            widened, widened, plain, widened, widened, plain,
            pltpu.VMEM(velocity.shape, f32),
            pltpu.VMEM((depth, ny, nz), f32),
            pltpu.VMEM((depth, 3 * rows, nz), f32),
            pltpu.VMEM((depth, rows, nz), f32),
            pltpu.VMEM((depth, rows, nz), f32),
            pltpu.SMEM(snap_of_step.shape, jnp.int32),
            pltpu.VMEM((snap_of_step.shape[1], 8, 128), f32),
            pltpu.VMEM((snap_of_step.shape[1], 8, 128), f32),
            dma((3,)), dma((4, 2, 2)), dma((4, 2, 2)), dma((fields, depth)), dma((fields, depth)), dma((4,)), dma((4,)),
            dma((slabs, 5)), dma((3, 5)), dma,
        ],
        compiler_params=pltpu.CompilerParams(
            collective_id=0, has_side_effects=True, vmem_limit_bytes=32 * 1024 * 1024),
        cost_estimate=pl.CostEstimate(flops=200 * state.size, bytes_accessed=28 * state.size, transcendentals=0),
    )(*(pltpu.with_memory_space_constraint(x, pltpu.HBM) for x in (state, velocity, snap_of_step)))
    final, gradient = written(final, gradient)
    return final[None], gradient


def solution(mesh):
    placed = (P("tm", None, "space", None, None), P(None, None, "space", None, None), P("tm", None))
    return jax.shard_map(
        functools.partial(body, mesh.shape["tm"], mesh.shape["space"]),
        mesh=mesh,
        in_specs=placed,
        out_specs=(P("tm", None, "space", None, None), P("space", "tm", None)),
        check_vma=False,
    )
```

```python
import functools

import jax
import jax.numpy as jnp
from jax import lax
from jax.experimental import pallas as pl
from jax.experimental.pallas import tpu as pltpu
from jax.sharding import PartitionSpec as P

coupling = 0.3
MESH = pl.DeviceIdType.MESH


def shifted(field):
    rows, lanes = field.shape
    row = lax.broadcasted_iota(jnp.int32, (8, lanes), 0)
    lane = lax.broadcasted_iota(jnp.int32, (rows, 128), 1)
    north = pltpu.roll(field, rows - 1, 0)
    north = jnp.concatenate([north[:-8], jnp.where(row == 7, 0.0, north[-8:])], axis=0)
    south = pltpu.roll(field, 1, 0)
    south = jnp.concatenate([jnp.where(row == 0, 0.0, south[:8]), south[8:]], axis=0)
    upper = pltpu.roll(field, lanes - 1, 1)
    upper = jnp.concatenate([upper[:, :-128], jnp.where(lane == 127, 0.0, upper[:, -128:])], axis=1)
    lower = pltpu.roll(field, 1, 1)
    lower = jnp.concatenate([jnp.where(lane == 0, 0.0, lower[:, :128]), lower[:, 128:]], axis=1)
    return north, south, upper, lower


def moved(west, centre, east, u, v, w, rate):
    north, south, upper, lower = shifted(centre)
    around = (east + west) + (north + south) + (upper + lower)
    transport = u * (east - west) + v * (north - south) + w * (upper - lower)
    return (1.0 - 6.0 * rate) * centre + rate * around + 0.25 * transport


def flow_at(flow, snap, layer):
    return tuple(flow[snap, c, layer] for c in range(3))


def flow_picked(flow, pick, layer):
    rows, lanes = flow.shape[3:]
    pick = jnp.concatenate([pick] * (lanes // pick.shape[1]), axis=1)
    pick = jnp.concatenate([pick] * (rows // pick.shape[0]), axis=0)
    return tuple(jnp.where(pick > 0.5, flow[1, c, layer], flow[0, c, layer]) for c in range(3))


def temper_step(src, flows, layer):
    a, b = src[0, layer + 1], src[1, layer + 1]
    return moved(src[0, layer], a, src[0, layer + 2], *flows, 0.14) + coupling * b


def dopant_step(src, flows, layer):
    return moved(src[1, layer], src[1, layer + 1], src[1, layer + 2], *flows, 0.06)


def kernel(
    slabs, blocks, state, velocity, snaps_in, out, grad,
    x0, x1, x2, y0, y1, y2, flow, total, from_mate, from_early, from_late, snaps, pick_out, pick,
    load_sem, halo_send, halo_recv, pass_send, pass_recv, raw_send, raw_recv, grad_send, grad_recv, out_sem,
):
    t, s = lax.axis_index("tm"), lax.axis_index("space")
    depth = x2.shape[1]
    pairs = depth // 2
    steps = snaps.shape[1]
    has_up, has_down = s < blocks - 1, s > 0
    first_phase, second_phase = t > 0, t < slabs - 1
    mate = t + 1 - 2 * lax.rem(t, 2)
    source = slabs // 2

    load_state = pltpu.make_async_copy(state, x0.at[:, pl.ds(1, depth)], load_sem.at[0])
    load_flow = pltpu.make_async_copy(velocity, flow, load_sem.at[1])
    load_snaps = pltpu.make_async_copy(snaps_in, snaps, load_sem.at[2])

    load_snaps.start()

    @pl.when(first_phase)
    def _():
        load_state.start()

    load_flow.start()

    barrier = pltpu.get_barrier_semaphore()

    def greet(target):
        pl.semaphore_signal(barrier, inc=1, device_id=target, device_id_type=MESH)

    for other in range(1, slabs):
        greet({"tm": lax.rem(t + other, slabs)})
    for by, there in ((1, has_up), (-1, has_down)):
        @pl.when(there)
        def _(by=by):
            greet({"space": s + by})
            pl.when(first_phase)(lambda: greet({"tm": t - 1, "space": s + by}))
            pl.when(second_phase)(lambda: greet({"tm": t + 1, "space": s + by}))

    sides = jnp.where(has_up, 1, 0) + jnp.where(has_down, 1, 0)
    rounds = 1 + jnp.where(first_phase, 1, 0) + jnp.where(second_phase, 1, 0)
    pl.semaphore_wait(barrier, slabs - 1 + sides * rounds)

    def halo(k, field, low, high, buf, tm=t):
        def copy(source, layer, side, by):
            return pltpu.make_async_remote_copy(
                source, buf.at[field, layer], halo_send.at[k, field, side], halo_recv.at[k, field, side],
                {"tm": tm, "space": s + by}, MESH)

        return copy(high, 0, 0, 1), copy(low, depth + 1, 1, -1)

    def send_halo(pair):
        pl.when(has_up)(lambda: pair[0].start())
        pl.when(has_down)(lambda: pair[1].start())

    def recv_halo(pair):
        pl.when(has_down)(lambda: pair[0].wait_recv())
        pl.when(has_up)(lambda: pair[1].wait_recv())

    def sent_halo(pair):
        pl.when(has_up)(lambda: pair[0].wait_send())
        pl.when(has_down)(lambda: pair[1].wait_send())

    def clear_ends(*bufs):
        for buf in bufs:
            @pl.when(s == 0)
            def _(buf=buf):
                buf[:, 0] = jnp.zeros(buf.shape[:1] + buf.shape[2:], jnp.float32)

            @pl.when(s == blocks - 1)
            def _(buf=buf):
                buf[:, depth + 1] = jnp.zeros(buf.shape[:1] + buf.shape[2:], jnp.float32)

    A, B = 0, 1
    halo0 = [halo(0, f, state.at[f, 0], state.at[f, depth - 1], x0) for f in (A, B)]
    halo1 = [halo(1, f, x1.at[f, 1], x1.at[f, depth], x1) for f in (A, B)]
    halo2 = [halo(2, f, x2.at[f, 0], x2.at[f, depth - 1], y0, (t - 1, mate)[f]) for f in (A, B)]
    halo3 = [halo(3, f, y1.at[f, 1], y1.at[f, depth], y1) for f in (A, B)]

    def passing(field, layer, target):
        return pltpu.make_async_remote_copy(
            x2.at[field, layer], y0.at[field, layer + 1], pass_send.at[field, layer], pass_recv.at[field, layer],
            {"tm": target}, MESH)

    def pass_pair(field, p, target):
        passing(field, p, target).start()
        passing(field, depth - 1 - p, target).start()

    def arrived(field, p, origin):
        passing(field, p, origin).wait_recv()
        passing(field, depth - 1 - p, origin).wait_recv()

    def half(part, layer, layers):
        there = x1.at[B, pl.ds(layer + 1, layers)]
        return pltpu.make_async_remote_copy(there, there, raw_send.at[part], raw_recv.at[part], {"tm": 0}, MESH)

    halves = [half(0, 0, 1), half(1, depth - 1, 1), half(2, 1, depth - 2)]
    send_pick = pltpu.make_async_remote_copy(pick_out, pick, raw_send.at[3], raw_recv.at[3], {"tm": 0}, MESH)

    def step_into(src, dst, offset, snap, p, summed=False):
        for layer in (p, depth - 1 - p):
            flows = flow_at(flow, snap, layer)
            temper = temper_step(src, flows, layer)
            dst[A, layer + offset] = temper
            dst[B, layer + offset] = dopant_step(src, flows, layer)
            if summed:
                total[layer] = src[A, layer + 1] + temper

    ends = (0, depth - 1)

    def end_dopant(src, dst, offset, snap):
        for layer in ends:
            dst[B, layer + offset] = dopant_step(src, flow_at(flow, snap, layer), layer)

    def end_temper(src, dst, offset, snap, summed=False):
        for layer in ends:
            temper = temper_step(src, flow_at(flow, snap, layer), layer)
            dst[A, layer + offset] = temper
            if summed:
                total[layer] = src[A, layer + 1] + temper

    @pl.when(first_phase)
    def _():
        send_halo(halo0[B])
        send_halo(halo0[A])

    load_snaps.wait()

    @pl.when(t == source)
    def _():
        pick_out[...] = jnp.full(pick_out.shape, snaps[0, 0].astype(jnp.float32))
        send_pick.start()

    clear_ends(x0, x1)
    pl.when(first_phase)(lambda: load_state.wait())
    load_flow.wait()

    @pl.when(t == 0)
    def _():
        def picked_step(layer):
            x2[B, layer] = dopant_step(x1, flow_picked(flow, pick[...], layer), layer)

        halves[0].wait_recv()
        halves[1].wait_recv()
        send_halo(halo1[B])
        send_pick.wait_recv()
        halves[2].wait_recv()

        @pl.loop(1, depth - 1)
        def _(layer):
            picked_step(layer)

        recv_halo(halo1[B])
        for layer in ends:
            picked_step(layer)
        send_halo(halo2[B])
        for p in range(pairs):
            pass_pair(B, p, mate)

    @pl.when(first_phase)
    def _():
        snap = snaps[0, steps - 1]

        @pl.loop(0, pairs - 1)
        def _(i):
            step_into(x0, x1, 1, snap, pairs - 1 - i)

        recv_halo(halo0[B])
        end_dopant(x0, x1, 1, snap)
        pl.when(t != source)(lambda: send_halo(halo1[B]))

        @pl.when(t == source)
        def _():
            for each in halves:
                each.start()

        recv_halo(halo0[A])
        end_temper(x0, x1, 1, snap)
        send_halo(halo1[A])
        snap = snaps[0, 0]

        @pl.loop(0, pairs - 1)
        def _(i):
            p = pairs - 1 - i
            for layer in (p, depth - 1 - p):
                temper = temper_step(x1, flow_at(flow, snap, layer), layer)
                x2[A, layer] = temper
                total[layer] = x1[A, layer + 1] + temper
            pass_pair(A, p, t - 1)

            @pl.when(t != source)
            def _():
                for layer in (p, depth - 1 - p):
                    x2[B, layer] = dopant_step(x1, flow_at(flow, snap, layer), layer)
                pass_pair(B, p, mate)

        @pl.when(t != source)
        def _():
            recv_halo(halo1[B])
            end_dopant(x1, x2, 0, snap)
            send_halo(halo2[B])
            pass_pair(B, 0, mate)

        recv_halo(halo1[A])
        end_temper(x1, x2, 0, snap, summed=True)
        send_halo(halo2[A])
        pass_pair(A, 0, t - 1)

    rows = total.shape[1] // slabs
    parts = ((2, depth - 4), (1, 1), (depth - 2, 1), (0, 1), (depth - 1, 1))
    inner, second, outer = (0,), (1, 2), (3, 4)

    class Share:
        def __init__(self, first, count, dst, slot, target):
            self.copies = [
                pltpu.make_async_remote_copy(
                    total.at[pl.ds(layer, layers), pl.ds(first * rows, count * rows)],
                    dst.at[pl.ds(layer, layers)], grad_send.at[target, part], grad_recv.at[slot, part],
                    {"tm": target}, MESH)
                for part, (layer, layers) in enumerate(parts)
            ]

        def start(self, which=inner + second + outer):
            for part in which:
                self.copies[part].start()

        def wait_recv(self):
            for copy in self.copies:
                copy.wait_recv()

        def wait_send(self):
            for copy in self.copies:
                copy.wait_send()

    mate0 = Share(1, 3, from_mate, 0, 1)
    mate3 = Share(0, 3, from_mate, 0, 2)
    back1 = Share(0, 1, from_late, 2, 0)
    back2 = Share(3, 1, from_late, 2, 3)
    cross20 = Share(0, 1, from_early, 1, 0)
    cross21 = Share(1, 1, from_early, 1, 1)
    cross12 = Share(2, 1, from_early, 1, 2)
    cross13 = Share(3, 1, from_early, 1, 3)

    def give(which):
        @pl.when(t == 0)
        def _():
            mate0.start(which)

        @pl.when(t == 1)
        def _():
            if which == inner:
                mate0.wait_recv()
            for layer, layers in (parts[part] for part in which):
                total[layer:layer + layers, rows:] += from_mate[layer:layer + layers]
            for each in (cross12, cross13, back1):
                each.start(which)

        @pl.when(t == 2)
        def _():
            if which == inner:
                mate3.wait_recv()
            for layer, layers in (parts[part] for part in which):
                total[layer:layer + layers, :3 * rows] += from_mate[layer:layer + layers]
            for each in (cross20, cross21, back2):
                each.start(which)

    pl.when(t == slabs - 1)(lambda: mate3.start())

    @pl.when(second_phase)
    def _():
        clear_ends(y0, y1)

        def ready(p):
            arrived(B, p, mate)
            arrived(A, p, t + 1)

        snap = snaps[0, steps - 1]
        ready(pairs - 1)

        @pl.loop(0, pairs - 2)
        def _(i):
            ready(pairs - 2 - i)
            step_into(y0, y1, 1, snap, pairs - 1 - i)

        arrived(B, 0, mate)
        recv_halo(halo2[B])
        end_dopant(y0, y1, 1, snap)
        send_halo(halo3[B])
        arrived(A, 0, t + 1)
        recv_halo(halo2[A])
        end_temper(y0, y1, 1, snap)
        send_halo(halo3[A])
        step_into(y0, y1, 1, snap, 1)
        snap = snaps[0, 0]

        @pl.loop(0, pairs - 1)
        def _(i):
            p = pairs - 1 - i
            step_into(y1, y2, 0, snap, p, summed=True)
            pl.when(p == 2)(lambda: give(inner))
            pl.when(p == 1)(lambda: give(second))

        recv_halo(halo3[B])
        end_dopant(y1, y2, 0, snap)
        recv_halo(halo3[A])
        end_temper(y1, y2, 0, snap, summed=True)
        give(outer)

    store_mid = pltpu.make_async_copy(y2, out, out_sem)
    store_end = pltpu.make_async_copy(x2, out, out_sem)
    pl.when(second_phase)(lambda: store_mid.start())
    pl.when(t == slabs - 1)(lambda: store_end.start())

    def mine(index):
        return total[:, index * rows:(index + 1) * rows]

    scale = 1.0 / steps

    @pl.when(t == 0)
    def _():
        cross20.wait_recv()
        back1.wait_recv()
        grad[...] = (mine(0) + from_late[...] + from_early[...]) * scale
        mate0.wait_send()

    @pl.when(t == 1)
    def _():
        cross21.wait_recv()
        grad[...] = (mine(1) + from_early[...]) * scale
        cross12.wait_send()
        cross13.wait_send()
        back1.wait_send()

    @pl.when(t == 2)
    def _():
        cross12.wait_recv()
        grad[...] = (mine(2) + from_early[...]) * scale
        cross20.wait_send()
        cross21.wait_send()
        back2.wait_send()

    @pl.when(t == 3)
    def _():
        back2.wait_recv()
        cross13.wait_recv()
        grad[...] = (mine(3) + from_late[...] + from_early[...]) * scale
        mate3.wait_send()

    @pl.when(t == source)
    def _():
        send_pick.wait_send()
        for each in halves:
            each.wait_send()

    @pl.when(first_phase)
    def _():
        for each in (halo0[A], halo0[B], halo1[A], halo2[A]):
            sent_halo(each)

        @pl.loop(0, depth)
        def _(layer):
            passing(A, layer, t - 1).wait_send()

    @pl.when(t != source)
    def _():
        sent_halo(halo1[B])
        sent_halo(halo2[B])

        @pl.loop(0, depth)
        def _(layer):
            passing(B, layer, mate).wait_send()

    @pl.when(second_phase)
    def _():
        sent_halo(halo3[A])
        sent_halo(halo3[B])
        store_mid.wait()

    pl.when(t == slabs - 1)(lambda: store_end.wait())


def write_kernel(final, grad, final_out, grad_out, sems):
    copies = [pltpu.make_async_copy(final, final_out, sems.at[0]), pltpu.make_async_copy(grad, grad_out, sems.at[1])]
    for each in copies:
        each.start()
    for each in copies:
        each.wait()


def written(final, gradient):
    return pl.pallas_call(
        write_kernel,
        out_shape=[jax.ShapeDtypeStruct(x.shape, x.dtype) for x in (final, gradient)],
        in_specs=[pl.BlockSpec(memory_space=pltpu.VMEM)] * 2,
        out_specs=[pl.BlockSpec(memory_space=pl.ANY)] * 2,
        scratch_shapes=[pltpu.SemaphoreType.DMA((2,))],
    )(*(pltpu.with_memory_space_constraint(x, pltpu.VMEM) for x in (final, gradient)))


def body(slabs, blocks, slab_states, velocity, snap_of_step):
    state = slab_states[0]
    fields, depth, ny, nz = state.shape
    rows = ny // slabs
    f32 = jnp.float32
    widened = pltpu.VMEM((fields, depth + 2, ny, nz), f32)
    plain = pltpu.VMEM((fields, depth, ny, nz), f32)
    dma = pltpu.SemaphoreType.DMA
    final, gradient = pl.pallas_call(
        functools.partial(kernel, slabs, blocks),
        out_shape=(
            jax.ShapeDtypeStruct(state.shape, f32),
            jax.ShapeDtypeStruct((depth, rows, nz), f32),
        ),
        in_specs=[
            pl.BlockSpec(memory_space=pltpu.HBM),
            pl.BlockSpec(memory_space=pltpu.HBM),
            pl.BlockSpec(memory_space=pltpu.HBM),
        ],
        out_specs=(pl.BlockSpec(memory_space=pl.ANY), pl.BlockSpec(memory_space=pltpu.VMEM)),
        scratch_shapes=[
            widened, widened, plain, widened, widened, plain,
            pltpu.VMEM(velocity.shape, f32),
            pltpu.VMEM((depth, ny, nz), f32),
            pltpu.VMEM((depth, 3 * rows, nz), f32),
            pltpu.VMEM((depth, rows, nz), f32),
            pltpu.VMEM((depth, rows, nz), f32),
            pltpu.SMEM(snap_of_step.shape, jnp.int32),
            pltpu.VMEM((8, 128), f32),
            pltpu.VMEM((8, 128), f32),
            dma((3,)), dma((4, 2, 2)), dma((4, 2, 2)), dma((fields, depth)), dma((fields, depth)), dma((4,)), dma((4,)),
            dma((slabs, 5)), dma((3, 5)), dma,
        ],
        compiler_params=pltpu.CompilerParams(
            collective_id=0, has_side_effects=True, vmem_limit_bytes=32 * 1024 * 1024),
        cost_estimate=pl.CostEstimate(flops=200 * state.size, bytes_accessed=28 * state.size, transcendentals=0),
    )(*(pltpu.with_memory_space_constraint(x, pltpu.HBM) for x in (state, velocity, snap_of_step)))
    final, gradient = written(final, gradient)
    return final[None], gradient


def solution(mesh):
    placed = (P("tm", None, "space", None, None), P(None, None, "space", None, None), P("tm", None))
    return jax.shard_map(
        functools.partial(body, mesh.shape["tm"], mesh.shape["space"]),
        mesh=mesh,
        in_specs=placed,
        out_specs=(P("tm", None, "space", None, None), P("space", "tm", None)),
        check_vma=False,
    )
```

```python
import functools

import jax
import jax.numpy as jnp
from jax import lax
from jax.experimental import pallas as pl
from jax.experimental.pallas import tpu as pltpu
from jax.sharding import PartitionSpec as P

coupling = 0.3
MESH = pl.DeviceIdType.MESH


def shifted(field):
    rows, lanes = field.shape
    row = lax.broadcasted_iota(jnp.int32, (8, lanes), 0)
    lane = lax.broadcasted_iota(jnp.int32, (rows, 128), 1)
    north = pltpu.roll(field, rows - 1, 0)
    north = jnp.concatenate([north[:-8], jnp.where(row == 7, 0.0, north[-8:])], axis=0)
    south = pltpu.roll(field, 1, 0)
    south = jnp.concatenate([jnp.where(row == 0, 0.0, south[:8]), south[8:]], axis=0)
    upper = pltpu.roll(field, lanes - 1, 1)
    upper = jnp.concatenate([upper[:, :-128], jnp.where(lane == 127, 0.0, upper[:, -128:])], axis=1)
    lower = pltpu.roll(field, 1, 1)
    lower = jnp.concatenate([jnp.where(lane == 0, 0.0, lower[:, :128]), lower[:, 128:]], axis=1)
    return north, south, upper, lower


def moved(west, centre, east, u, v, w, rate):
    north, south, upper, lower = shifted(centre)
    around = (east + west) + (north + south) + (upper + lower)
    transport = u * (east - west) + v * (north - south) + w * (upper - lower)
    return (1.0 - 6.0 * rate) * centre + rate * around + 0.25 * transport


def flow_at(flow, snap, layer):
    return tuple(flow[snap, c, layer] for c in range(3))


def flow_picked(flow, pick, layer):
    rows, lanes = flow.shape[3:]
    pick = jnp.concatenate([pick] * (lanes // pick.shape[1]), axis=1)
    pick = jnp.concatenate([pick] * (rows // pick.shape[0]), axis=0)
    return tuple(jnp.where(pick > 0.5, flow[1, c, layer], flow[0, c, layer]) for c in range(3))


def temper_step(src, flows, layer):
    a, b = src[0, layer + 1], src[1, layer + 1]
    return moved(src[0, layer], a, src[0, layer + 2], *flows, 0.14) + coupling * b


def dopant_step(src, flows, layer):
    return moved(src[1, layer], src[1, layer + 1], src[1, layer + 2], *flows, 0.06)


def kernel(
    slabs, blocks, state, velocity, snaps_in, out, grad,
    x0, x1, x2, y0, y1, y2, flow, total, from_mate, from_early, from_late, snaps, pick_out, pick,
    load_sem, halo_send, halo_recv, pass_send, pass_recv, raw_send, raw_recv, grad_send, grad_recv, out_sem,
):
    t, s = lax.axis_index("tm"), lax.axis_index("space")
    depth = x2.shape[1]
    pairs = depth // 2
    steps = snaps.shape[1]
    has_up, has_down = s < blocks - 1, s > 0
    first_phase, second_phase = t > 0, t < slabs - 1
    mate = t + 1 - 2 * lax.rem(t, 2)
    source = slabs // 2

    load_state = pltpu.make_async_copy(state, x0.at[:, pl.ds(1, depth)], load_sem.at[0])
    load_flow = pltpu.make_async_copy(velocity, flow, load_sem.at[1])
    load_snaps = pltpu.make_async_copy(snaps_in, snaps, load_sem.at[2])

    load_snaps.start()

    @pl.when(first_phase)
    def _():
        load_state.start()

    load_flow.start()

    barrier = pltpu.get_barrier_semaphore()

    def greet(target):
        pl.semaphore_signal(barrier, inc=1, device_id=target, device_id_type=MESH)

    for other in range(1, slabs):
        greet({"tm": lax.rem(t + other, slabs)})
    for by, there in ((1, has_up), (-1, has_down)):
        @pl.when(there)
        def _(by=by):
            greet({"space": s + by})
            pl.when(first_phase)(lambda: greet({"tm": t - 1, "space": s + by}))
            pl.when(second_phase)(lambda: greet({"tm": t + 1, "space": s + by}))

    sides = jnp.where(has_up, 1, 0) + jnp.where(has_down, 1, 0)
    rounds = 1 + jnp.where(first_phase, 1, 0) + jnp.where(second_phase, 1, 0)
    pl.semaphore_wait(barrier, slabs - 1 + sides * rounds)

    def halo(k, field, low, high, buf, tm=t):
        def copy(source, layer, side, by):
            return pltpu.make_async_remote_copy(
                source, buf.at[field, layer], halo_send.at[k, field, side], halo_recv.at[k, field, side],
                {"tm": tm, "space": s + by}, MESH)

        return copy(high, 0, 0, 1), copy(low, depth + 1, 1, -1)

    def send_halo(pair):
        pl.when(has_up)(lambda: pair[0].start())
        pl.when(has_down)(lambda: pair[1].start())

    def recv_halo(pair):
        pl.when(has_down)(lambda: pair[0].wait_recv())
        pl.when(has_up)(lambda: pair[1].wait_recv())

    def sent_halo(pair):
        pl.when(has_up)(lambda: pair[0].wait_send())
        pl.when(has_down)(lambda: pair[1].wait_send())

    def clear_ends(*bufs):
        for buf in bufs:
            @pl.when(s == 0)
            def _(buf=buf):
                buf[:, 0] = jnp.zeros(buf.shape[:1] + buf.shape[2:], jnp.float32)

            @pl.when(s == blocks - 1)
            def _(buf=buf):
                buf[:, depth + 1] = jnp.zeros(buf.shape[:1] + buf.shape[2:], jnp.float32)

    A, B = 0, 1
    halo0 = [halo(0, f, state.at[f, 0], state.at[f, depth - 1], x0) for f in (A, B)]
    halo1 = [halo(1, f, x1.at[f, 1], x1.at[f, depth], x1) for f in (A, B)]
    halo2 = [halo(2, f, x2.at[f, 0], x2.at[f, depth - 1], y0, (t - 1, mate)[f]) for f in (A, B)]
    halo3 = [halo(3, f, y1.at[f, 1], y1.at[f, depth], y1) for f in (A, B)]

    def passing(field, layer, target):
        return pltpu.make_async_remote_copy(
            x2.at[field, layer], y0.at[field, layer + 1], pass_send.at[field, layer], pass_recv.at[field, layer],
            {"tm": target}, MESH)

    def pass_pair(field, p, target):
        passing(field, p, target).start()
        passing(field, depth - 1 - p, target).start()

    def arrived(field, p, origin):
        passing(field, p, origin).wait_recv()
        passing(field, depth - 1 - p, origin).wait_recv()

    def half(part, layer, layers):
        there = x1.at[B, pl.ds(layer + 1, layers)]
        return pltpu.make_async_remote_copy(there, there, raw_send.at[part], raw_recv.at[part], {"tm": 0}, MESH)

    halves = [half(0, 0, 1), half(1, depth - 1, 1), half(2, 1, depth - 2)]
    send_pick = pltpu.make_async_remote_copy(pick_out, pick, raw_send.at[3], raw_recv.at[3], {"tm": 0}, MESH)

    def step_into(src, dst, offset, snap, p, summed=False):
        for layer in (p, depth - 1 - p):
            flows = flow_at(flow, snap, layer)
            temper = temper_step(src, flows, layer)
            dst[A, layer + offset] = temper
            dst[B, layer + offset] = dopant_step(src, flows, layer)
            if summed:
                total[layer] = src[A, layer + 1] + temper

    ends = (0, depth - 1)

    def end_dopant(src, dst, offset, snap):
        for layer in ends:
            dst[B, layer + offset] = dopant_step(src, flow_at(flow, snap, layer), layer)

    def end_temper(src, dst, offset, snap, summed=False):
        for layer in ends:
            temper = temper_step(src, flow_at(flow, snap, layer), layer)
            dst[A, layer + offset] = temper
            if summed:
                total[layer] = src[A, layer + 1] + temper

    @pl.when(first_phase)
    def _():
        send_halo(halo0[B])
        send_halo(halo0[A])

    load_snaps.wait()

    @pl.when(t == source)
    def _():
        pick_out[...] = jnp.full(pick_out.shape, snaps[0, 0].astype(jnp.float32))
        send_pick.start()

    clear_ends(x0, x1)
    pl.when(first_phase)(lambda: load_state.wait())
    load_flow.wait()

    @pl.when(t == 0)
    def _():
        def picked_step(layer):
            x2[B, layer] = dopant_step(x1, flow_picked(flow, pick[...], layer), layer)

        halves[0].wait_recv()
        halves[1].wait_recv()
        send_halo(halo1[B])
        send_pick.wait_recv()
        halves[2].wait_recv()

        @pl.loop(1, depth - 1)
        def _(layer):
            picked_step(layer)

        recv_halo(halo1[B])
        for layer in ends:
            picked_step(layer)
        send_halo(halo2[B])
        for p in range(pairs):
            pass_pair(B, p, mate)

    @pl.when(first_phase)
    def _():
        snap = snaps[0, steps - 1]

        @pl.loop(0, pairs - 1)
        def _(i):
            step_into(x0, x1, 1, snap, pairs - 1 - i)

        pl.when(t == source)(lambda: halves[2].start())
        recv_halo(halo0[B])
        end_dopant(x0, x1, 1, snap)
        pl.when(t != source)(lambda: send_halo(halo1[B]))

        @pl.when(t == source)
        def _():
            for each in halves[:2]:
                each.start()

        recv_halo(halo0[A])
        end_temper(x0, x1, 1, snap)
        send_halo(halo1[A])
        snap = snaps[0, 0]

        @pl.loop(0, pairs - 1)
        def _(i):
            p = pairs - 1 - i
            for layer in (p, depth - 1 - p):
                temper = temper_step(x1, flow_at(flow, snap, layer), layer)
                x2[A, layer] = temper
                total[layer] = x1[A, layer + 1] + temper
            pass_pair(A, p, t - 1)

            @pl.when(t != source)
            def _():
                for layer in (p, depth - 1 - p):
                    x2[B, layer] = dopant_step(x1, flow_at(flow, snap, layer), layer)
                pass_pair(B, p, mate)

        @pl.when(t != source)
        def _():
            recv_halo(halo1[B])
            end_dopant(x1, x2, 0, snap)
            send_halo(halo2[B])
            pass_pair(B, 0, mate)

        recv_halo(halo1[A])
        end_temper(x1, x2, 0, snap, summed=True)
        send_halo(halo2[A])
        pass_pair(A, 0, t - 1)

    rows = total.shape[1] // slabs
    parts = ((2, depth - 4), (1, 1), (depth - 2, 1), (0, 1), (depth - 1, 1))
    inner, second, outer = (0,), (1, 2), (3, 4)

    class Share:
        def __init__(self, first, count, dst, slot, target):
            self.copies = [
                pltpu.make_async_remote_copy(
                    total.at[pl.ds(layer, layers), pl.ds(first * rows, count * rows)],
                    dst.at[pl.ds(layer, layers)], grad_send.at[target, part], grad_recv.at[slot, part],
                    {"tm": target}, MESH)
                for part, (layer, layers) in enumerate(parts)
            ]

        def start(self, which=inner + second + outer):
            for part in which:
                self.copies[part].start()

        def wait_recv(self):
            for copy in self.copies:
                copy.wait_recv()

        def wait_send(self):
            for copy in self.copies:
                copy.wait_send()

    mate0 = Share(1, 3, from_mate, 0, 1)
    mate3 = Share(0, 3, from_mate, 0, 2)
    back1 = Share(0, 1, from_late, 2, 0)
    back2 = Share(3, 1, from_late, 2, 3)
    cross20 = Share(0, 1, from_early, 1, 0)
    cross21 = Share(1, 1, from_early, 1, 1)
    cross12 = Share(2, 1, from_early, 1, 2)
    cross13 = Share(3, 1, from_early, 1, 3)

    def give(which):
        @pl.when(t == 0)
        def _():
            mate0.start(which)

        @pl.when(t == 1)
        def _():
            if which == inner:
                mate0.wait_recv()
            for layer, layers in (parts[part] for part in which):
                total[layer:layer + layers, rows:] += from_mate[layer:layer + layers]
            for each in (cross12, cross13, back1):
                each.start(which)

        @pl.when(t == 2)
        def _():
            if which == inner:
                mate3.wait_recv()
            for layer, layers in (parts[part] for part in which):
                total[layer:layer + layers, :3 * rows] += from_mate[layer:layer + layers]
            for each in (cross20, cross21, back2):
                each.start(which)

    pl.when(t == slabs - 1)(lambda: mate3.start())

    @pl.when(second_phase)
    def _():
        clear_ends(y0, y1)

        def ready(p):
            arrived(B, p, mate)
            arrived(A, p, t + 1)

        snap = snaps[0, steps - 1]
        ready(1)
        arrived(B, 0, mate)
        recv_halo(halo2[B])
        end_dopant(y0, y1, 1, snap)
        send_halo(halo3[B])
        arrived(A, 0, t + 1)
        recv_halo(halo2[A])
        end_temper(y0, y1, 1, snap)
        send_halo(halo3[A])

        for p in range(2, pairs):
            ready(p)

        @pl.loop(0, pairs - 1)
        def _(i):
            step_into(y0, y1, 1, snap, pairs - 1 - i)

        snap = snaps[0, 0]

        @pl.loop(0, pairs - 1)
        def _(i):
            p = pairs - 1 - i
            step_into(y1, y2, 0, snap, p, summed=True)
            pl.when(p == 2)(lambda: give(inner))
            pl.when(p == 1)(lambda: give(second))

        recv_halo(halo3[B])
        end_dopant(y1, y2, 0, snap)
        recv_halo(halo3[A])
        end_temper(y1, y2, 0, snap, summed=True)
        give(outer)

    store_mid = pltpu.make_async_copy(y2, out, out_sem)
    store_end = pltpu.make_async_copy(x2, out, out_sem)
    pl.when(second_phase)(lambda: store_mid.start())
    pl.when(t == slabs - 1)(lambda: store_end.start())

    def mine(index):
        return total[:, index * rows:(index + 1) * rows]

    scale = 1.0 / steps

    @pl.when(t == 0)
    def _():
        cross20.wait_recv()
        back1.wait_recv()
        grad[...] = (mine(0) + from_late[...] + from_early[...]) * scale
        mate0.wait_send()

    @pl.when(t == 1)
    def _():
        cross21.wait_recv()
        grad[...] = (mine(1) + from_early[...]) * scale
        cross12.wait_send()
        cross13.wait_send()
        back1.wait_send()

    @pl.when(t == 2)
    def _():
        cross12.wait_recv()
        grad[...] = (mine(2) + from_early[...]) * scale
        cross20.wait_send()
        cross21.wait_send()
        back2.wait_send()

    @pl.when(t == 3)
    def _():
        back2.wait_recv()
        cross13.wait_recv()
        grad[...] = (mine(3) + from_late[...] + from_early[...]) * scale
        mate3.wait_send()

    @pl.when(t == source)
    def _():
        send_pick.wait_send()
        for each in halves:
            each.wait_send()

    @pl.when(first_phase)
    def _():
        for each in (halo0[A], halo0[B], halo1[A], halo2[A]):
            sent_halo(each)

        @pl.loop(0, depth)
        def _(layer):
            passing(A, layer, t - 1).wait_send()

    @pl.when(t != source)
    def _():
        sent_halo(halo1[B])
        sent_halo(halo2[B])

        @pl.loop(0, depth)
        def _(layer):
            passing(B, layer, mate).wait_send()

    @pl.when(second_phase)
    def _():
        sent_halo(halo3[A])
        sent_halo(halo3[B])
        store_mid.wait()

    pl.when(t == slabs - 1)(lambda: store_end.wait())


def write_kernel(final, grad, final_out, grad_out, sems):
    copies = [pltpu.make_async_copy(final, final_out, sems.at[0]), pltpu.make_async_copy(grad, grad_out, sems.at[1])]
    for each in copies:
        each.start()
    for each in copies:
        each.wait()


def written(final, gradient):
    return pl.pallas_call(
        write_kernel,
        out_shape=[jax.ShapeDtypeStruct(x.shape, x.dtype) for x in (final, gradient)],
        in_specs=[pl.BlockSpec(memory_space=pltpu.VMEM)] * 2,
        out_specs=[pl.BlockSpec(memory_space=pl.ANY)] * 2,
        scratch_shapes=[pltpu.SemaphoreType.DMA((2,))],
    )(*(pltpu.with_memory_space_constraint(x, pltpu.VMEM) for x in (final, gradient)))


def body(slabs, blocks, slab_states, velocity, snap_of_step):
    state = slab_states[0]
    fields, depth, ny, nz = state.shape
    rows = ny // slabs
    f32 = jnp.float32
    widened = pltpu.VMEM((fields, depth + 2, ny, nz), f32)
    plain = pltpu.VMEM((fields, depth, ny, nz), f32)
    dma = pltpu.SemaphoreType.DMA
    final, gradient = pl.pallas_call(
        functools.partial(kernel, slabs, blocks),
        out_shape=(
            jax.ShapeDtypeStruct(state.shape, f32),
            jax.ShapeDtypeStruct((depth, rows, nz), f32),
        ),
        in_specs=[
            pl.BlockSpec(memory_space=pltpu.HBM),
            pl.BlockSpec(memory_space=pltpu.HBM),
            pl.BlockSpec(memory_space=pltpu.HBM),
        ],
        out_specs=(pl.BlockSpec(memory_space=pl.ANY), pl.BlockSpec(memory_space=pltpu.VMEM)),
        scratch_shapes=[
            widened, widened, plain, widened, widened, plain,
            pltpu.VMEM(velocity.shape, f32),
            pltpu.VMEM((depth, ny, nz), f32),
            pltpu.VMEM((depth, 3 * rows, nz), f32),
            pltpu.VMEM((depth, rows, nz), f32),
            pltpu.VMEM((depth, rows, nz), f32),
            pltpu.SMEM(snap_of_step.shape, jnp.int32),
            pltpu.VMEM((8, 128), f32),
            pltpu.VMEM((8, 128), f32),
            dma((3,)), dma((4, 2, 2)), dma((4, 2, 2)), dma((fields, depth)), dma((fields, depth)), dma((4,)), dma((4,)),
            dma((slabs, 5)), dma((3, 5)), dma,
        ],
        compiler_params=pltpu.CompilerParams(
            collective_id=0, has_side_effects=True, vmem_limit_bytes=32 * 1024 * 1024),
        cost_estimate=pl.CostEstimate(flops=200 * state.size, bytes_accessed=28 * state.size, transcendentals=0),
    )(*(pltpu.with_memory_space_constraint(x, pltpu.HBM) for x in (state, velocity, snap_of_step)))
    final, gradient = written(final, gradient)
    return final[None], gradient


def solution(mesh):
    placed = (P("tm", None, "space", None, None), P(None, None, "space", None, None), P("tm", None))
    return jax.shard_map(
        functools.partial(body, mesh.shape["tm"], mesh.shape["space"]),
        mesh=mesh,
        in_specs=placed,
        out_specs=(P("tm", None, "space", None, None), P("space", "tm", None)),
        check_vma=False,
    )
```

```python
import functools

import jax
import jax.numpy as jnp
from jax import lax
from jax.experimental import pallas as pl
from jax.experimental.pallas import tpu as pltpu
from jax.sharding import PartitionSpec as P

coupling = 0.3
MESH = pl.DeviceIdType.MESH


def shifted(field):
    rows, lanes = field.shape
    row = lax.broadcasted_iota(jnp.int32, (8, lanes), 0)
    lane = lax.broadcasted_iota(jnp.int32, (rows, 128), 1)
    north = pltpu.roll(field, rows - 1, 0)
    north = jnp.concatenate([north[:-8], jnp.where(row == 7, 0.0, north[-8:])], axis=0)
    south = pltpu.roll(field, 1, 0)
    south = jnp.concatenate([jnp.where(row == 0, 0.0, south[:8]), south[8:]], axis=0)
    upper = pltpu.roll(field, lanes - 1, 1)
    upper = jnp.concatenate([upper[:, :-128], jnp.where(lane == 127, 0.0, upper[:, -128:])], axis=1)
    lower = pltpu.roll(field, 1, 1)
    lower = jnp.concatenate([jnp.where(lane == 0, 0.0, lower[:, :128]), lower[:, 128:]], axis=1)
    return north, south, upper, lower


def moved(west, centre, east, u, v, w, rate):
    north, south, upper, lower = shifted(centre)
    around = (east + west) + (north + south) + (upper + lower)
    transport = u * (east - west) + v * (north - south) + w * (upper - lower)
    return (1.0 - 6.0 * rate) * centre + rate * around + 0.25 * transport


def flow_at(flow, snap, layer):
    return tuple(flow[snap, c, layer] for c in range(3))


def flow_picked(flow, pick, layer):
    rows, lanes = flow.shape[3:]
    pick = jnp.concatenate([pick] * (lanes // pick.shape[1]), axis=1)
    pick = jnp.concatenate([pick] * (rows // pick.shape[0]), axis=0)
    return tuple(jnp.where(pick > 0.5, flow[1, c, layer], flow[0, c, layer]) for c in range(3))


def temper_step(src, flows, layer):
    a, b = src[0, layer + 1], src[1, layer + 1]
    return moved(src[0, layer], a, src[0, layer + 2], *flows, 0.14) + coupling * b


def dopant_step(src, flows, layer):
    return moved(src[1, layer], src[1, layer + 1], src[1, layer + 2], *flows, 0.06)


def kernel(
    slabs, blocks, state, velocity, snaps_in, out, grad,
    x0, x1, x2, y0, y1, y2, flow, total, from_mate, from_early, from_late, snaps, pick_out, pick,
    load_sem, halo_send, halo_recv, pass_send, pass_recv, raw_send, raw_recv, grad_send, grad_recv, out_sem,
):
    t, s = lax.axis_index("tm"), lax.axis_index("space")
    depth = x2.shape[1]
    pairs = depth // 2
    steps = snaps.shape[1]
    has_up, has_down = s < blocks - 1, s > 0
    first_phase, second_phase = t > 0, t < slabs - 1
    mate = t + 1 - 2 * lax.rem(t, 2)
    source = slabs // 2

    load_state = pltpu.make_async_copy(state, x0.at[:, pl.ds(1, depth)], load_sem.at[0])
    load_flow = pltpu.make_async_copy(velocity, flow, load_sem.at[1])
    load_snaps = pltpu.make_async_copy(snaps_in, snaps, load_sem.at[2])

    load_snaps.start()

    @pl.when(first_phase)
    def _():
        load_state.start()

    load_flow.start()

    barrier = pltpu.get_barrier_semaphore()

    def greet(target):
        pl.semaphore_signal(barrier, inc=1, device_id=target, device_id_type=MESH)

    for other in range(1, slabs):
        greet({"tm": lax.rem(t + other, slabs)})
    for by, there in ((1, has_up), (-1, has_down)):
        @pl.when(there)
        def _(by=by):
            greet({"space": s + by})
            pl.when(first_phase)(lambda: greet({"tm": t - 1, "space": s + by}))
            pl.when(second_phase)(lambda: greet({"tm": t + 1, "space": s + by}))

    sides = jnp.where(has_up, 1, 0) + jnp.where(has_down, 1, 0)
    rounds = 1 + jnp.where(first_phase, 1, 0) + jnp.where(second_phase, 1, 0)
    pl.semaphore_wait(barrier, slabs - 1 + sides * rounds)

    def halo(k, field, low, high, buf, tm=t):
        def copy(source, layer, side, by):
            return pltpu.make_async_remote_copy(
                source, buf.at[field, layer], halo_send.at[k, field, side], halo_recv.at[k, field, side],
                {"tm": tm, "space": s + by}, MESH)

        return copy(high, 0, 0, 1), copy(low, depth + 1, 1, -1)

    def send_halo(pair):
        pl.when(has_up)(lambda: pair[0].start())
        pl.when(has_down)(lambda: pair[1].start())

    def recv_halo(pair):
        pl.when(has_down)(lambda: pair[0].wait_recv())
        pl.when(has_up)(lambda: pair[1].wait_recv())

    def sent_halo(pair):
        pl.when(has_up)(lambda: pair[0].wait_send())
        pl.when(has_down)(lambda: pair[1].wait_send())

    def clear_ends(*bufs):
        for buf in bufs:
            @pl.when(s == 0)
            def _(buf=buf):
                buf[:, 0] = jnp.zeros(buf.shape[:1] + buf.shape[2:], jnp.float32)

            @pl.when(s == blocks - 1)
            def _(buf=buf):
                buf[:, depth + 1] = jnp.zeros(buf.shape[:1] + buf.shape[2:], jnp.float32)

    A, B = 0, 1
    halo0 = [halo(0, f, state.at[f, 0], state.at[f, depth - 1], x0) for f in (A, B)]
    halo1 = [halo(1, f, x1.at[f, 1], x1.at[f, depth], x1) for f in (A, B)]
    halo2 = [halo(2, f, x2.at[f, 0], x2.at[f, depth - 1], y0, (t - 1, mate)[f]) for f in (A, B)]
    halo3 = [halo(3, f, y1.at[f, 1], y1.at[f, depth], y1) for f in (A, B)]

    def passing(field, layer, target):
        return pltpu.make_async_remote_copy(
            x2.at[field, layer], y0.at[field, layer + 1], pass_send.at[field, layer], pass_recv.at[field, layer],
            {"tm": target}, MESH)

    def pass_pair(field, p, target):
        passing(field, p, target).start()
        passing(field, depth - 1 - p, target).start()

    def arrived(field, p, origin):
        passing(field, p, origin).wait_recv()
        passing(field, depth - 1 - p, origin).wait_recv()

    def half(part, layer, layers):
        there = x1.at[B, pl.ds(layer + 1, layers)]
        return pltpu.make_async_remote_copy(there, there, raw_send.at[part], raw_recv.at[part], {"tm": 0}, MESH)

    halves = [half(0, 0, 1), half(1, depth - 1, 1), half(2, 1, depth - 2)]
    send_pick = pltpu.make_async_remote_copy(pick_out, pick, raw_send.at[3], raw_recv.at[3], {"tm": 0}, MESH)

    def step_into(src, dst, offset, snap, p, summed=False):
        for layer in (p, depth - 1 - p):
            flows = flow_at(flow, snap, layer)
            temper = temper_step(src, flows, layer)
            dst[A, layer + offset] = temper
            dst[B, layer + offset] = dopant_step(src, flows, layer)
            if summed:
                total[layer] = src[A, layer + 1] + temper

    ends = (0, depth - 1)

    def end_dopant(src, dst, offset, snap):
        for layer in ends:
            dst[B, layer + offset] = dopant_step(src, flow_at(flow, snap, layer), layer)

    def end_temper(src, dst, offset, snap, summed=False):
        for layer in ends:
            temper = temper_step(src, flow_at(flow, snap, layer), layer)
            dst[A, layer + offset] = temper
            if summed:
                total[layer] = src[A, layer + 1] + temper

    @pl.when(first_phase)
    def _():
        send_halo(halo0[B])
        send_halo(halo0[A])

    load_snaps.wait()

    @pl.when(t == source)
    def _():
        pick_out[...] = jnp.full(pick_out.shape, snaps[0, 0].astype(jnp.float32))
        send_pick.start()

    clear_ends(x0, x1)
    pl.when(first_phase)(lambda: load_state.wait())
    load_flow.wait()

    @pl.when(t == 0)
    def _():
        def picked_step(layer):
            x2[B, layer] = dopant_step(x1, flow_picked(flow, pick[...], layer), layer)

        halves[0].wait_recv()
        halves[1].wait_recv()
        send_halo(halo1[B])
        send_pick.wait_recv()
        halves[2].wait_recv()

        @pl.loop(1, depth - 1)
        def _(layer):
            picked_step(layer)

        recv_halo(halo1[B])
        for layer in ends:
            picked_step(layer)
        send_halo(halo2[B])
        for p in range(pairs):
            pass_pair(B, p, mate)

    @pl.when(first_phase)
    def _():
        snap = snaps[0, steps - 1]

        @pl.loop(0, pairs - 1)
        def _(i):
            step_into(x0, x1, 1, snap, pairs - 1 - i)

        recv_halo(halo0[B])
        end_dopant(x0, x1, 1, snap)
        pl.when(t != source)(lambda: send_halo(halo1[B]))

        @pl.when(t == source)
        def _():
            for each in halves:
                each.start()

        recv_halo(halo0[A])
        end_temper(x0, x1, 1, snap)
        send_halo(halo1[A])
        snap = snaps[0, 0]

        @pl.loop(0, pairs - 1)
        def _(i):
            p = pairs - 1 - i
            for layer in (p, depth - 1 - p):
                temper = temper_step(x1, flow_at(flow, snap, layer), layer)
                x2[A, layer] = temper
                total[layer] = x1[A, layer + 1] + temper
            pass_pair(A, p, t - 1)

            @pl.when(t != source)
            def _():
                for layer in (p, depth - 1 - p):
                    x2[B, layer] = dopant_step(x1, flow_at(flow, snap, layer), layer)
                pass_pair(B, p, mate)

        @pl.when(t != source)
        def _():
            recv_halo(halo1[B])
            end_dopant(x1, x2, 0, snap)
            send_halo(halo2[B])
            pass_pair(B, 0, mate)

        recv_halo(halo1[A])
        end_temper(x1, x2, 0, snap, summed=True)
        send_halo(halo2[A])
        pass_pair(A, 0, t - 1)

    rows = total.shape[1] // slabs
    parts = ((2, depth - 4), (1, 1), (depth - 2, 1), (0, 1), (depth - 1, 1))
    inner, second, outer = (0,), (1, 2), (3, 4)

    class Share:
        def __init__(self, first, count, dst, slot, target):
            self.copies = [
                pltpu.make_async_remote_copy(
                    total.at[pl.ds(layer, layers), pl.ds(first * rows, count * rows)],
                    dst.at[pl.ds(layer, layers)], grad_send.at[target, part], grad_recv.at[slot, part],
                    {"tm": target}, MESH)
                for part, (layer, layers) in enumerate(parts)
            ]

        def start(self, which=inner + second + outer):
            for part in which:
                self.copies[part].start()

        def wait_recv(self):
            for copy in self.copies:
                copy.wait_recv()

        def wait_send(self):
            for copy in self.copies:
                copy.wait_send()

    mate0 = Share(1, 3, from_mate, 0, 1)
    mate3 = Share(0, 3, from_mate, 0, 2)
    back1 = Share(0, 1, from_late, 2, 0)
    back2 = Share(3, 1, from_late, 2, 3)
    cross20 = Share(0, 1, from_early, 1, 0)
    cross21 = Share(1, 1, from_early, 1, 1)
    cross12 = Share(2, 1, from_early, 1, 2)
    cross13 = Share(3, 1, from_early, 1, 3)

    def give(which):
        @pl.when(t == 0)
        def _():
            mate0.start(which)

        @pl.when(t == 1)
        def _():
            if which == inner:
                mate0.wait_recv()
            for layer, layers in (parts[part] for part in which):
                total[layer:layer + layers, rows:] += from_mate[layer:layer + layers]
            for each in (cross12, cross13, back1):
                each.start(which)

        @pl.when(t == 2)
        def _():
            if which == inner:
                mate3.wait_recv()
            for layer, layers in (parts[part] for part in which):
                total[layer:layer + layers, :3 * rows] += from_mate[layer:layer + layers]
            for each in (cross20, cross21, back2):
                each.start(which)

    pl.when(t == slabs - 1)(lambda: mate3.start())

    @pl.when(second_phase)
    def _():
        clear_ends(y0, y1)

        def ready(p):
            arrived(B, p, mate)
            arrived(A, p, t + 1)

        snap = snaps[0, steps - 1]
        ready(1)
        arrived(B, 0, mate)
        recv_halo(halo2[B])
        end_dopant(y0, y1, 1, snap)
        send_halo(halo3[B])
        arrived(A, 0, t + 1)
        recv_halo(halo2[A])
        end_temper(y0, y1, 1, snap)
        send_halo(halo3[A])

        for p in range(2, pairs):
            ready(p)

        @pl.loop(0, pairs - 1)
        def _(i):
            step_into(y0, y1, 1, snap, pairs - 1 - i)

        snap = snaps[0, 0]

        @pl.loop(0, pairs - 1)
        def _(i):
            p = pairs - 1 - i
            step_into(y1, y2, 0, snap, p, summed=True)
            pl.when(p == 2)(lambda: give(inner))
            pl.when(p == 1)(lambda: give(second))

        recv_halo(halo3[B])
        end_dopant(y1, y2, 0, snap)
        recv_halo(halo3[A])
        end_temper(y1, y2, 0, snap, summed=True)
        give(outer)

    store_mid = pltpu.make_async_copy(y2, out, out_sem)
    store_end = pltpu.make_async_copy(x2, out, out_sem)
    pl.when(second_phase)(lambda: store_mid.start())
    pl.when(t == slabs - 1)(lambda: store_end.start())

    def mine(index):
        return total[:, index * rows:(index + 1) * rows]

    scale = 1.0 / steps

    @pl.when(t == 0)
    def _():
        cross20.wait_recv()
        back1.wait_recv()
        grad[...] = (mine(0) + from_late[...] + from_early[...]) * scale
        mate0.wait_send()

    @pl.when(t == 1)
    def _():
        cross21.wait_recv()
        grad[...] = (mine(1) + from_early[...]) * scale
        cross12.wait_send()
        cross13.wait_send()
        back1.wait_send()

    @pl.when(t == 2)
    def _():
        cross12.wait_recv()
        grad[...] = (mine(2) + from_early[...]) * scale
        cross20.wait_send()
        cross21.wait_send()
        back2.wait_send()

    @pl.when(t == 3)
    def _():
        back2.wait_recv()
        cross13.wait_recv()
        grad[...] = (mine(3) + from_late[...] + from_early[...]) * scale
        mate3.wait_send()

    @pl.when(t == source)
    def _():
        send_pick.wait_send()
        for each in halves:
            each.wait_send()

    @pl.when(first_phase)
    def _():
        for each in (halo0[A], halo0[B], halo1[A], halo2[A]):
            sent_halo(each)

        @pl.loop(0, depth)
        def _(layer):
            passing(A, layer, t - 1).wait_send()

    @pl.when(t != source)
    def _():
        sent_halo(halo1[B])
        sent_halo(halo2[B])

        @pl.loop(0, depth)
        def _(layer):
            passing(B, layer, mate).wait_send()

    @pl.when(second_phase)
    def _():
        sent_halo(halo3[A])
        sent_halo(halo3[B])
        store_mid.wait()

    pl.when(t == slabs - 1)(lambda: store_end.wait())


def write_kernel(final, grad, final_out, grad_out, sems):
    copies = [pltpu.make_async_copy(final, final_out, sems.at[0]), pltpu.make_async_copy(grad, grad_out, sems.at[1])]
    for each in copies:
        each.start()
    for each in copies:
        each.wait()


def written(final, gradient):
    return pl.pallas_call(
        write_kernel,
        out_shape=[jax.ShapeDtypeStruct(x.shape, x.dtype) for x in (final, gradient)],
        in_specs=[pl.BlockSpec(memory_space=pltpu.VMEM)] * 2,
        out_specs=[pl.BlockSpec(memory_space=pl.ANY)] * 2,
        scratch_shapes=[pltpu.SemaphoreType.DMA((2,))],
    )(*(pltpu.with_memory_space_constraint(x, pltpu.VMEM) for x in (final, gradient)))


def body(slabs, blocks, slab_states, velocity, snap_of_step):
    state = slab_states[0]
    fields, depth, ny, nz = state.shape
    rows = ny // slabs
    f32 = jnp.float32
    widened = pltpu.VMEM((fields, depth + 2, ny, nz), f32)
    plain = pltpu.VMEM((fields, depth, ny, nz), f32)
    dma = pltpu.SemaphoreType.DMA
    final, gradient = pl.pallas_call(
        functools.partial(kernel, slabs, blocks),
        out_shape=(
            jax.ShapeDtypeStruct(state.shape, f32),
            jax.ShapeDtypeStruct((depth, rows, nz), f32),
        ),
        in_specs=[
            pl.BlockSpec(memory_space=pltpu.HBM),
            pl.BlockSpec(memory_space=pltpu.HBM),
            pl.BlockSpec(memory_space=pltpu.HBM),
        ],
        out_specs=(pl.BlockSpec(memory_space=pl.ANY), pl.BlockSpec(memory_space=pltpu.VMEM)),
        scratch_shapes=[
            widened, widened, plain, widened, widened, plain,
            pltpu.VMEM(velocity.shape, f32),
            pltpu.VMEM((depth, ny, nz), f32),
            pltpu.VMEM((depth, 3 * rows, nz), f32),
            pltpu.VMEM((depth, rows, nz), f32),
            pltpu.VMEM((depth, rows, nz), f32),
            pltpu.SMEM(snap_of_step.shape, jnp.int32),
            pltpu.VMEM((8, 128), f32),
            pltpu.VMEM((8, 128), f32),
            dma((3,)), dma((4, 2, 2)), dma((4, 2, 2)), dma((fields, depth)), dma((fields, depth)), dma((4,)), dma((4,)),
            dma((slabs, 5)), dma((3, 5)), dma,
        ],
        compiler_params=pltpu.CompilerParams(
            collective_id=0, has_side_effects=True, vmem_limit_bytes=32 * 1024 * 1024),
        cost_estimate=pl.CostEstimate(flops=200 * state.size, bytes_accessed=28 * state.size, transcendentals=0),
    )(*(pltpu.with_memory_space_constraint(x, pltpu.HBM) for x in (state, velocity, snap_of_step)))
    final, gradient = written(final, gradient)
    return final[None], gradient


def solution(mesh):
    placed = (P("tm", None, "space", None, None), P(None, None, "space", None, None), P("tm", None))
    return jax.shard_map(
        functools.partial(body, mesh.shape["tm"], mesh.shape["space"]),
        mesh=mesh,
        in_specs=placed,
        out_specs=(P("tm", None, "space", None, None), P("space", "tm", None)),
        check_vma=False,
    )
```
